32 devices in a mesh: dom: 4 (over x, core), block: 8 (over z, y).
Axes of the slice: x: 2, y: 2, z: 4, core: 2. Of those that a mesh axis runs over, the one named last changes fastest.
Arguments:
- entities: float32 [1024, 400], P(('dom', 'block')), may hold values from -2.5 to 2.5
- relations: float32 [4096, 400], replicated, may hold values from -4 to 4
- src_index: int32 [4, 16, 256], P('dom', 'block'), may hold values from 0 to 255
- dst_index: int32 [4, 16, 256], P('dom', 'block'), may hold values from 0 to 255
- rel_index: int32 [4, 16, 256], P('dom', 'block'), may hold values from 0 to 4095
- neg_index: int32 [4, 16, 1024], P('dom', 'block'), may hold values from 0 to 255
- counts: int32 [4, 16], P('dom', 'block'), may hold values from 1 to 256, 2048 in all within a row
- edge_weight: float32 [4, 16, 256], P('dom', 'block'), may hold values from 0.25 to 4
Outputs:
- entity_grad: float32 [1024, 400], P(('dom', 'block'))
- relation_grad: float32 [4096, 400], replicated
The draws below stay inside these ranges and needn't reach their ends.
Inputs may be any that keep to these rules, and one draw needn't show every extreme that they name: The counts of one bucket sum to 2048.
All inputs are finite; a program needn't handle non-finite values. No bound on the sum of `counts` on one device may be relied on, other than what follows from the above.
Results may differ from the reference program's by a relative error of at most 0.0003.
Values sent between devices are 32-bit elements; how exact they have to be, the bound alone decides.
No kernel may reach another device: no remote copies, remote signals or barrier semaphores. Data moves between devices by JAX's collectives and lax.ppermute only.
A program may use at most 128 MiB of HBM per device.

```python
import math
import jax
import jax.numpy as jnp
import numpy as np
from jax import lax

DIM = 400
NREL = 4096
EDGES = 256
NEG = 1024
PART_ROWS = 256
N_ENT = 1024
GROUP_BLOCKS = 16
N_DOM = 4


def plant(values, stream_key, low, top_value):
    spot = [jax.random.randint(jax.random.fold_in(stream_key, axis), (), 0, length) for axis, length in enumerate(values.shape)]
    widest = values.shape.index(max(values.shape))
    beside = spot[:widest] + [(spot[widest] + 1) % values.shape[widest]] + spot[widest + 1:]
    return values.at[tuple(spot)].set(low).at[tuple(beside)].set(top_value)


def level_of(rng, shape, split, smallest, top_value):
    def one(position, shards_of):
        draws = jax.random.uniform(jax.random.fold_in(jax.random.fold_in(rng, 6), position), (shards_of,), jnp.float32, smallest / len(split), top_value / len(split))
        return jnp.repeat(jnp.exp(draws), shape[position] // shards_of).reshape((-1,) + (1,) * (len(shape) - position - 1))

    level = one(*split[0])
    for cut in split[1:]:
        level = level * one(*cut)
    return level


def rank_bounds(amount, skew):
    loads = [(1 << 20) // math.isqrt(standing ** skew) + 1 for standing in range(1, amount + 1)]
    spread = 1 + sum(loads) // (1 << 30)
    return np.cumsum(np.array([max(1, weight // spread) for weight in loads]))


def ranked_ids(key, shape, count, lean):
    grid = rank_bounds(count, lean)
    lot = jax.random.randint(jax.random.fold_in(key, 1), shape, 0, int(grid[count - 1]))
    rank = jnp.searchsorted(jnp.asarray(grid, jnp.int32), lot, side="right")
    return jax.random.permutation(jax.random.fold_in(key, 2), count)[rank].astype(jnp.int32)


def profile(count, total, bound, lean):
    loads = [(1 << 20) // math.isqrt(standing ** lean) + 1 for standing in range(2, count + 1)]
    surplus, given = total - bound - (count - 1), [1] * (count - 1)
    while surplus > 0:
        free = [i for i in range(count - 1) if given[i] < bound]
        whole, remaining = sum([loads[i] for i in free]), surplus
        for i in free:
            extra = min(bound - given[i], max(1, remaining * loads[i] // whole), surplus)
            given[i] = given[i] + extra
            surplus = surplus - extra
    return np.array([bound] + given)


def ragged_sizes(key, amount, total, most, skew):
    if amount == 2:
        one = jax.random.randint(key, (), max(1, total - most), min(most, total - 1) + 1)
        return jnp.stack([one, total - one])
    lengths = jnp.asarray(profile(amount, total, most, skew), jnp.int32)
    couples = (amount - 1) // 2
    source_of, taker = lengths[1:1 + 2 * couples:2], lengths[2:2 + 2 * couples:2]
    margin = jnp.minimum(source_of - 1, most - taker)
    moved = jax.random.randint(jax.random.fold_in(key, 1), (couples,), 0, 1 << 20) % (margin + 1)
    lengths = lengths.at[1:1 + 2 * couples:2].set(source_of - moved).at[2:2 + 2 * couples:2].set(taker + moved)
    return lengths[jax.random.permutation(jax.random.fold_in(key, 2), amount)]


def scatter_about(own_key, shape, width, bound, cuts=(), kind=jnp.bfloat16):
    result = width * jax.random.normal(own_key, shape, jnp.float32)
    if cuts:
        result = result * level_of(own_key, shape, cuts, -0.22, 0.18)
    return jnp.clip(result, -bound, bound).astype(kind)


def setup_inputs(seed: int = 0) -> dict:
    seeds = jax.random.split(jax.random.key(seed), 9)
    entities = scatter_about(seeds[0], (N_ENT, DIM), 0.3, 2.5, ((0, 32),), jnp.float32)
    relations = scatter_about(seeds[1], (NREL, DIM), 0.5, 4.0, (), jnp.float32)
    src_index = plant(jax.random.randint(seeds[2], (N_DOM, GROUP_BLOCKS, EDGES), 0, PART_ROWS), jax.random.fold_in(seeds[2], 1), 0, PART_ROWS - 1).astype(jnp.int32)
    dst_index = plant(jax.random.randint(seeds[3], (N_DOM, GROUP_BLOCKS, EDGES), 0, PART_ROWS), jax.random.fold_in(seeds[3], 1), 0, PART_ROWS - 1).astype(jnp.int32)
    rel_index = plant(ranked_ids(seeds[4], (N_DOM, GROUP_BLOCKS, EDGES), NREL, 2), jax.random.fold_in(seeds[4], 3), 0, NREL - 1).astype(jnp.int32)
    neg_index = plant(jax.random.randint(seeds[5], (N_DOM, GROUP_BLOCKS, NEG), 0, PART_ROWS), jax.random.fold_in(seeds[5], 1), 0, PART_ROWS - 1).astype(jnp.int32)
    counts = jax.vmap(lambda own: ragged_sizes(own, GROUP_BLOCKS, GROUP_BLOCKS * EDGES // 2, EDGES, 2))(jax.random.split(seeds[6], N_DOM)).reshape((N_DOM, GROUP_BLOCKS)).astype(jnp.int32)
    edge_weight = jnp.clip(jnp.exp(math.log(4.0) - 2.7725887 * jax.random.uniform(seeds[7], (N_DOM, GROUP_BLOCKS, EDGES), jnp.float32) ** level_of(seeds[7], (N_DOM, GROUP_BLOCKS, EDGES), ((0, 4), (1, 8)), -0.2, 0.2)), 0.25, 4.0)
    return dict(entities=entities, relations=relations, src_index=src_index, dst_index=dst_index, rel_index=rel_index, neg_index=neg_index, counts=counts, edge_weight=edge_weight)


def block_gradients(source_rows, target_rows, relations, source_ids, target_ids, relation_ids, negative_ids, live_count, edge_weight):
    half_width = source_rows.shape[1] // 2
    sources = source_rows[source_ids]
    targets = target_rows[target_ids]
    factors = relations[relation_ids]
    negatives = target_rows[negative_ids]
    source_real, source_imag = sources[:, :half_width], sources[:, half_width:]
    factor_real, factor_imag = factors[:, :half_width], factors[:, half_width:]
    queries = jnp.concatenate([source_real * factor_real - source_imag * factor_imag, source_real * factor_imag + source_imag * factor_real], axis=1)
    positive = jnp.sum(queries * targets, axis=1)
    negative = jnp.dot(queries, negatives.T, precision=lax.Precision.HIGHEST, preferred_element_type=jnp.float32)
    live_mask = (jnp.arange(queries.shape[0], dtype=jnp.int32) < live_count).astype(jnp.float32)
    scaled = edge_weight * live_mask
    negative_count = negatives.shape[0]
    grad_positive = -jax.nn.sigmoid(-positive) * scaled
    grad_negative = jax.nn.sigmoid(negative) * (scaled / negative_count)[:, None]
    grad_query = grad_positive[:, None] * targets + jnp.dot(grad_negative, negatives, precision=lax.Precision.HIGHEST, preferred_element_type=jnp.float32)
    grad_target = grad_positive[:, None] * queries
    grad_drawn = jnp.dot(grad_negative.T, queries, precision=lax.Precision.HIGHEST, preferred_element_type=jnp.float32)
    query_real, query_imag = grad_query[:, :half_width], grad_query[:, half_width:]
    grad_source = jnp.concatenate([query_real * factor_real + query_imag * factor_imag, query_imag * factor_real - query_real * factor_imag], axis=1)
    grad_factor = jnp.concatenate([query_real * source_real + query_imag * source_imag, query_imag * source_real - query_real * source_imag], axis=1)
    return grad_source, grad_target, grad_drawn, grad_factor


def reference(entities, relations, src_index, dst_index, rel_index, neg_index, counts, edge_weight):
    pieces = [entities[part * PART_ROWS:(part + 1) * PART_ROWS] for part in range(N_DOM)]
    totals = [jnp.zeros((PART_ROWS, DIM), jnp.float32) for part in range(N_DOM)]
    relation_total = jnp.zeros((NREL, DIM), jnp.float32)
    for part in range(N_DOM):
        partner = part ^ (N_DOM // 2)
        source_rows = pieces[part]
        target_rows = pieces[partner]

        def one_block(carry, inputs):
            source_total, target_total, relation_acc = carry
            source_ids, target_ids, relation_ids, negative_ids, live_count, weights = inputs
            grad_source, grad_target, grad_drawn, grad_factor = block_gradients(source_rows, target_rows, relations, source_ids, target_ids, relation_ids, negative_ids, live_count, weights)
            source_total = source_total.at[source_ids].add(grad_source)
            target_total = target_total.at[target_ids].add(grad_target).at[negative_ids].add(grad_drawn)
            relation_acc = relation_acc.at[relation_ids].add(grad_factor)
            return (source_total, target_total, relation_acc), None

        start = (jnp.zeros((PART_ROWS, DIM), jnp.float32), jnp.zeros((PART_ROWS, DIM), jnp.float32), relation_total)
        (source_total, target_total, relation_total), unused = lax.scan(one_block, start, (src_index[part], dst_index[part], rel_index[part], neg_index[part], counts[part], edge_weight[part]))
        totals[part] = totals[part] + source_total
        totals[partner] = totals[partner] + target_total
    return jnp.concatenate(totals, axis=0), relation_total
```

```python
import functools

import jax
import jax.numpy as jnp
from jax import lax
from jax.experimental import pallas as pl
from jax.experimental.pallas import tpu as pltpu
from jax.sharding import PartitionSpec as P

LANES = 128
CHUNK = 128
LANE_TILES = 4
VMEM_BYTES = 58 * 1024 * 1024


def swap(x, axis, bit):
    count = lax.axis_size(axis)
    return lax.ppermute(x, axis, [(i, i ^ (1 << bit)) for i in range(count)])


def gather_all(x, stages):
    for axis, bit in stages:
        x = jnp.concatenate([x, swap(x, axis, bit)], axis=0)
    return x


def table_kernel(half, rel_ref, out_ref):
    width = LANE_TILES // 2 * LANES
    count = rel_ref.shape[1]
    for part in range(2):
        rows = rel_ref[part * half : (part + 1) * half, :]
        rows = jnp.concatenate([rows, jnp.zeros((width - half, count), jnp.float32)], axis=0)
        rows = rows.T
        for j in range(LANE_TILES // 2):
            out_ref[:, part * (LANE_TILES // 2) + j, :] = rows[:, j * LANES : (j + 1) * LANES]


def relation_table(relations):
    count, dim = relations.shape
    step = 512
    return pl.pallas_call(
        functools.partial(table_kernel, dim // 2),
        grid=(count // step,),
        in_specs=[pl.BlockSpec((dim, step), lambda i: (0, i))],
        out_specs=pl.BlockSpec((step, LANE_TILES, LANES), lambda i: (i, 0, 0)),
        out_shape=jax.ShapeDtypeStruct((count, LANE_TILES, LANES), jnp.float32),
        name="relation_table",
    )(relations.T)


def high_low(x):
    high = x.astype(jnp.bfloat16)
    return high, (x - high.astype(jnp.float32)).astype(jnp.bfloat16)


def dot(a, b):
    return jnp.dot(a, b, preferred_element_type=jnp.float32)


def spread(j, places):
    out = 0
    for bit, place in enumerate(places):
        out = out | (((j >> bit) & 1) << place)
    return out


def main_kernel(
    spec,
    rel_ids,
    live,
    where,
    table,
    first,
    second,
    counts_of,
    out_ref,
    ent_ref,
    *scratch,
):
    (half, rows, shards, blocks, edges, places_a, places_b, place_a, place_b) = spec
    accs = scratch[:-7]
    ent, both, high_t, low_t, factor, grads, mine = scratch[-7:]
    width = LANE_TILES // 2 * LANES
    part_rows = rows * shards
    me, side = where[0], where[1]

    def clear(i, carry):
        at = pl.ds(i * 8, 8)
        for acc in accs:
            acc[at] = jnp.zeros((8,) + acc.shape[1:], jnp.float32)
        return carry

    lax.fori_loop(0, accs[0].shape[0] // 8, clear, 0)
    mine[...] = jnp.zeros_like(mine)

    for x in range(2):
        for j in range(shards):
            ka = spread(j, places_a) | (x << place_a)
            kb = spread(j, places_b) | (x << place_b)
            at = pl.ds(pl.multiple_of((j ^ me) * rows, 8), rows)
            ent[x, at, :width] = first[ka, :rows, :]
            ent[x, at, width:] = second[kb, :rows, :]
        whole = ent[x]
        high, low = high_low(whole)
        both[x, :, : 2 * width] = high
        both[x, :, 2 * width :] = low
        high, low = high_low(whole.T)
        high_t[x] = high
        low_t[x] = low

    own = me * rows

    def block(t, carry):
        bucket, rest = t // (shards * blocks), t % (shards * blocks)
        shard, slot = rest // blocks, rest % blocks
        x = bucket ^ side
        j = shard ^ me
        ka = spread(j, places_a) | (x << place_a)
        kb = spread(j, places_b) | (x << place_b)
        count = live[kb * blocks + slot]

        def chunk(s, carry):
            base = s * CHUNK
            id_base = (ka * blocks + slot) * edges + base

            def fetch(g, carry):
                for u in range(8):
                    e = g * 8 + u
                    factor[e] = table[rel_ids[id_base + e]]
                return carry

            lax.fori_loop(0, CHUNK // 8, fetch, 0)

            at = pl.ds(pl.multiple_of(base, CHUNK), CHUNK)
            tile = first[ka, pl.ds(rows, 4 * blocks), at]

            def chosen(k):
                row = tile[k * blocks : k * blocks + 1]
                for i in range(1, blocks):
                    row = jnp.where(slot == i, tile[k * blocks + i : k * blocks + i + 1], row)
                return row

            infos = [chosen(0), chosen(1), chosen(3)]
            source_row = infos[0].astype(jnp.int32)
            columns = jnp.concatenate(infos + [jnp.zeros((5, CHUNK), jnp.float32)], axis=0).T
            source_col = columns[:, 0:1].astype(jnp.int32)
            target_col = columns[:, 1:2].astype(jnp.int32)
            weight_col = columns[:, 2:3]

            lane = lax.broadcasted_iota(jnp.int32, (CHUNK, part_rows), 1)
            pick = jnp.where(source_col == lane, 1.0, 0.0).astype(jnp.bfloat16)
            sources = dot(pick, both[x])
            sources = sources[:, : 2 * width] + sources[:, 2 * width :]
            s_re, s_im = sources[:, :width], sources[:, width:]
            w = [factor[:, q, :] for q in range(LANE_TILES)]
            w_re, w_im = jnp.concatenate(w[:2], axis=1), jnp.concatenate(w[2:], axis=1)
            queries = jnp.concatenate([s_re * w_re - s_im * w_im, s_re * w_im + s_im * w_re], axis=1)
            q_high, q_low = high_low(queries)
            scores = dot(q_high, high_t[1 - x]) + (dot(q_high, low_t[1 - x]) + dot(q_low, high_t[1 - x]))

            small = jnp.exp(-jnp.abs(scores))
            near = 1.0 / (1.0 + small)
            far = small * near
            up = scores >= 0.0
            sig = jnp.where(up, near, far)
            sig_neg = jnp.where(up, far, near)
            g = sig * counts_of[kb * blocks + slot] - jnp.where(target_col == lane, sig_neg, 0.0)
            g = g * weight_col
            g_high, g_low = high_low(g)
            gq = dot(g_high, both[1 - x])
            gq = gq[:, : 2 * width] + (gq[:, 2 * width :] + dot(g_low, both[1 - x, :, : 2 * width]))
            g_re, g_im = gq[:, :width], gq[:, width:]
            gw = [g_re * s_re + g_im * s_im, g_im * s_re - g_re * s_im]
            for q in range(LANE_TILES):
                grads[:, q, :] = gw[q // 2][:, (q % 2) * LANES : (q % 2 + 1) * LANES]

            @pl.when(x == 0)
            def _():
                gs = jnp.concatenate([g_re * w_re + g_im * w_im, g_im * w_re - g_re * w_im], axis=1)
                sub = lax.broadcasted_iota(jnp.int32, (rows, CHUNK), 0)
                back = jnp.where(source_row - own == sub, 1.0, 0.0).astype(jnp.bfloat16)
                s_high, s_low = high_low(gs)
                mine[...] += dot(back, s_high) + dot(back, s_low)

            @pl.when(x == 1)
            def _():
                flipped = scratch_rows(g, own)
                f_high, f_low = high_low(flipped)
                mine[...] += dot(f_high, q_high) + (dot(f_high, q_low) + dot(f_low, q_high))

            groups = (jnp.minimum(count - base, CHUNK) + 7) // 8

            def push(n, carry):
                for u in range(8):
                    e = n * 8 + u
                    r = rel_ids[id_base + e]
                    acc = accs[u % len(accs)]
                    acc[r] = acc[r] + grads[e]
                return carry

            lax.fori_loop(0, groups, push, 0)
            return carry

        def scratch_rows(g, own):
            select = jnp.where(
                lax.broadcasted_iota(jnp.int32, (part_rows, LANES), 0)
                == own + lax.broadcasted_iota(jnp.int32, (part_rows, LANES), 1),
                1.0,
                0.0,
            ).astype(jnp.bfloat16)
            high, low = high_low(g)
            picked = dot(high, select) + dot(low, select)
            return picked.T[:rows]

        return lax.fori_loop(0, (count + CHUNK - 1) // CHUNK, chunk, carry)

    lax.fori_loop(0, 2 * shards * blocks, block, 0)

    ent_ref[:, :half] = mine[:, :half]
    ent_ref[:, half:] = mine[:, width : width + half]

    def finish(i, carry):
        at = pl.ds(pl.multiple_of(i * LANES, LANES), LANES)
        for q in range(LANE_TILES):
            total = accs[0][at, q, :]
            for acc in accs[1:]:
                total = total + acc[at, q, :]
            low = (q // 2) * half + (q % 2) * LANES
            size = min(LANES, half - (q % 2) * LANES)
            out_ref[low : low + size, at] = total.T[:size]
        return carry

    lax.fori_loop(0, out_ref.shape[1] // LANES, finish, 0)


def body(entities, relations, src_index, dst_index, rel_index, neg_index, counts, edge_weight):
    rows, dim = entities.shape
    half = dim // 2
    width = LANE_TILES // 2 * LANES
    relation_count = relations.shape[0]
    blocks, edges = src_index.shape[1:]
    dom_count, shards = lax.axis_size("dom"), lax.axis_size("block")
    part_rows = rows * shards
    partner_bit = dom_count.bit_length() - 2
    block_bits = shards.bit_length() - 1
    other_bits = [bit for bit in range(dom_count.bit_length() - 1) if bit != partner_bit]

    table = relation_table(relations)

    real = jnp.pad(entities[:, :half], ((0, 0), (0, width - half)))
    imag = jnp.pad(entities[:, half:], ((0, 0), (0, width - half)))
    alive = jnp.arange(edges, dtype=jnp.int32)[None, :] < counts[0][:, None]
    weight = edge_weight[0] * alive.astype(jnp.float32)
    entity_ids = jnp.arange(part_rows, dtype=jnp.int32)
    times = jnp.sum((neg_index[0][:, :, None] == entity_ids).astype(jnp.float32), axis=1)
    times = times / neg_index.shape[2]
    ids = jnp.concatenate([src_index[0], dst_index[0], rel_index[0]], axis=0).astype(jnp.float32)
    info_a = jnp.concatenate([ids, weight], axis=0).reshape(-1, width)
    live_row = jnp.pad(counts[0].astype(jnp.float32)[None, :], ((0, 0), (0, width - blocks)))
    times_rows = blocks * part_rows // width
    info_b = jnp.concatenate([times.reshape(-1, width), live_row], axis=0)
    info_b = jnp.pad(info_b, ((0, -info_b.shape[0] % 8), (0, 0)))

    upper = [("block", bit) for bit in reversed(range(1, block_bits))]
    stages_a = upper + [("dom", partner_bit), ("block", 0)]
    stages_b = upper + [("block", 0), ("dom", partner_bit)]
    first = gather_all(jnp.concatenate([real, info_a], axis=0)[None], stages_a)
    second = gather_all(jnp.concatenate([imag, info_b], axis=0)[None], stages_b)
    places_a = tuple(stages_a.index(("block", bit)) for bit in range(block_bits))
    places_b = tuple(stages_b.index(("block", bit)) for bit in range(block_bits))
    place_a, place_b = stages_a.index(("dom", partner_bit)), stages_b.index(("dom", partner_bit))

    id_rows = blocks * edges // width
    rel_ids = first[:, rows + 2 * id_rows : rows + 3 * id_rows, :].astype(jnp.int32).reshape(-1)
    live = second[:, rows + times_rows, :blocks].astype(jnp.int32).reshape(-1)
    times_all = second[:, rows : rows + times_rows, :].reshape(-1, 1, part_rows)
    where = jnp.stack([lax.axis_index("block"), (lax.axis_index("dom") >> partner_bit) & 1]).astype(jnp.int32)

    sums = 4 if part_rows <= 256 else 2
    spec = (half, rows, shards, blocks, edges, places_a, places_b, place_a, place_b)
    smem = pl.BlockSpec(memory_space=pltpu.SMEM)
    vmem = pl.BlockSpec(memory_space=pltpu.VMEM)
    relation_part, entity_grad = pl.pallas_call(
        functools.partial(main_kernel, spec),
        in_specs=[smem, smem, smem, vmem, vmem, vmem, vmem],
        out_specs=(vmem, vmem),
        out_shape=(
            jax.ShapeDtypeStruct((dim, relation_count), jnp.float32),
            jax.ShapeDtypeStruct((rows, dim), jnp.float32),
        ),
        scratch_shapes=[pltpu.VMEM((relation_count, LANE_TILES, LANES), jnp.float32)] * sums
        + [
            pltpu.VMEM((2, part_rows, 2 * width), jnp.float32),
            pltpu.VMEM((2, part_rows, 4 * width), jnp.bfloat16),
            pltpu.VMEM((2, 2 * width, part_rows), jnp.bfloat16),
            pltpu.VMEM((2, 2 * width, part_rows), jnp.bfloat16),
            pltpu.VMEM((CHUNK, LANE_TILES, LANES), jnp.float32),
            pltpu.VMEM((CHUNK, LANE_TILES, LANES), jnp.float32),
            pltpu.VMEM((rows, 2 * width), jnp.float32),
        ],
        compiler_params=pltpu.CompilerParams(vmem_limit_bytes=VMEM_BYTES),
        name="gradients",
    )(rel_ids, live, where, table, first, second, times_all)

    for bit in other_bits:
        relation_part = relation_part + swap(relation_part, "dom", bit)
    return entity_grad, relation_part.T


def solution(mesh):
    placed = (
        P(("dom", "block"), None),
        P(),
        P("dom", "block", None),
        P("dom", "block", None),
        P("dom", "block", None),
        P("dom", "block", None),
        P("dom", "block"),
        P("dom", "block", None),
    )
    return jax.shard_map(
        body,
        mesh=mesh,
        in_specs=placed,
        out_specs=(P(("dom", "block"), None), P()),
        check_vma=False,
    )
```

```python
import functools

import jax
import jax.numpy as jnp
from jax import lax
from jax.experimental import pallas as pl
from jax.experimental.pallas import tpu as pltpu
from jax.sharding import PartitionSpec as P

LANES = 128
CHUNK = 256
LANE_TILES = 4
VMEM_BYTES = 58 * 1024 * 1024


def swap(x, axis, bit):
    count = lax.axis_size(axis)
    return lax.ppermute(x, axis, [(i, i ^ (1 << bit)) for i in range(count)])


def gather_all(x, stages):
    for axis, bit in stages:
        x = jnp.concatenate([x, swap(x, axis, bit)], axis=0)
    return x


def table_kernel(half, rel_ref, out_ref):
    width = LANE_TILES // 2 * LANES
    count = rel_ref.shape[1]
    flat = out_ref.reshape(count * LANE_TILES, LANES)
    for part in range(2):
        rows = rel_ref[part * half : (part + 1) * half, :]
        rows = jnp.concatenate([rows, jnp.zeros((width - half, count), jnp.float32)], axis=0)
        rows = rows.T
        for j in range(LANE_TILES // 2):
            at = pl.ds(part * (LANE_TILES // 2) + j, count, stride=LANE_TILES)
            flat[at, :] = rows[:, j * LANES : (j + 1) * LANES]


def relation_table(relations):
    count, dim = relations.shape
    step = 512
    return pl.pallas_call(
        functools.partial(table_kernel, dim // 2),
        grid=(count // step,),
        in_specs=[pl.BlockSpec((dim, step), lambda i: (0, i))],
        out_specs=pl.BlockSpec((step, LANE_TILES, LANES), lambda i: (i, 0, 0)),
        out_shape=jax.ShapeDtypeStruct((count, LANE_TILES, LANES), jnp.float32),
        name="relation_table",
    )(relations.T)


def high_low(x):
    high = x.astype(jnp.bfloat16)
    return high, (x - high.astype(jnp.float32)).astype(jnp.bfloat16)


def dot(a, b):
    return jnp.dot(a, b, preferred_element_type=jnp.float32)


def spread(j, places):
    out = 0
    for bit, place in enumerate(places):
        out = out | (((j >> bit) & 1) << place)
    return out


def tiles(ref, low, count, q):
    flat = ref.reshape(ref.shape[0] * ref.shape[1], LANES)
    return flat[pl.ds(low * LANE_TILES + q, count, stride=LANE_TILES), :]


def main_kernel(
    spec,
    live,
    where,
    table,
    first,
    second,
    counts_of,
    out_ref,
    ent_ref,
    *scratch,
):
    (half, rows, shards, blocks, edges, places_a, places_b, place_a, place_b) = spec
    accs = scratch[:-12]
    (ent, stack, stack_t, times, info, ids_v, ids, factor, grads, flip, mine, seg) = scratch[-12:]
    width = LANE_TILES // 2 * LANES
    part_rows = rows * shards
    group = shards * blocks
    total = group * edges // 2
    relation_count = out_ref.shape[1]
    me, side = where[0], where[1]
    own = me * rows

    def clear(i, carry):
        at = pl.ds(i * 8, 8)
        for acc in accs:
            acc[at] = jnp.zeros((8,) + acc.shape[1:], jnp.float32)
        return carry

    lax.fori_loop(0, relation_count // 8, clear, 0)
    mine[...] = jnp.zeros_like(mine)
    info[...] = jnp.zeros_like(info)

    for x in range(2):
        for j in range(shards):
            ka = spread(j, places_a) | (x << place_a)
            kb = spread(j, places_b) | (x << place_b)
            at = pl.ds(pl.multiple_of((j ^ me) * rows, 8), rows)
            ent[at, :width] = first[ka, :rows, :]
            ent[at, width:] = second[kb, :rows, :]
        whole = ent[...]
        high, low = high_low(whole)
        stack[x] = jnp.concatenate([high, low, high], axis=0)
        high, low = high_low(whole.T)
        stack_t[x] = jnp.concatenate([high, low, high], axis=0)

    def place(n, x):
        j = (n // blocks) ^ me
        ka = spread(j, places_a) | (x << place_a)
        kb = spread(j, places_b) | (x << place_b)
        return ka, kb, n % blocks

    for x in range(2):
        rows_of = []
        for n in range(group):
            ka, kb, slot = place(n, x)
            rows_of.append(counts_of[kb * blocks + slot])
        high, low = high_low(jnp.concatenate(rows_of, axis=0))
        times[x] = jnp.concatenate([high, low], axis=0)

        def lay(n, offset):
            ka, kb, slot = place(n, x)
            count = live[kb * blocks + slot]
            tile = first[ka, pl.ds(rows, 4 * blocks), :]

            def chosen(k):
                row = tile[k * blocks : k * blocks + 1]
                for i in range(1, blocks):
                    row = jnp.where(slot == i, tile[k * blocks + i : k * blocks + i + 1], row)
                return row

            number = jnp.zeros((1, edges), jnp.float32) + n.astype(jnp.float32)
            data = [chosen(k) for k in range(4)] + [number, jnp.zeros((3, edges), jnp.float32)]
            data = jnp.concatenate(data, axis=0)
            data = jnp.where(lax.broadcasted_iota(jnp.int32, data.shape, 1) < count, data, 0.0)
            data = jnp.concatenate([data, jnp.zeros((8, LANES), jnp.float32)], axis=1)
            data = pltpu.roll(data, offset % LANES, 1)
            at = pl.ds(pl.multiple_of((offset // LANES) * LANES, LANES), edges + LANES)
            info[x, :, at] = info[x, :, at] + data
            return offset + count

        lax.fori_loop(0, group, lay, jnp.int32(0))
        for i in range(total // LANES):
            ids_v[x, i : i + 1, :] = info[x, 2:3, i * LANES : (i + 1) * LANES].astype(jnp.int32)

    move = pltpu.make_async_copy(ids_v, ids, seg)
    move.start()
    move.wait()

    def row_id(x, at):
        return ids[x, at // LANES, at % LANES]

    def compute(x, start):
        at = pl.ds(pl.multiple_of(start, CHUNK), CHUNK)
        data = info[x, :, at]
        columns = data.T
        source_row = data[0:1].astype(jnp.int32)
        source_col = columns[:, 0:1].astype(jnp.int32)
        target_col = columns[:, 1:2].astype(jnp.int32)
        weight_col = columns[:, 3:4]
        block_col = columns[:, 4:5].astype(jnp.int32)

        lane = lax.broadcasted_iota(jnp.int32, (CHUNK, part_rows), 1)
        pick = jnp.where(source_col == lane, 1.0, 0.0).astype(jnp.bfloat16)
        sources = dot(jnp.concatenate([pick, pick], axis=1), stack[x, : 2 * part_rows])
        s_re, s_im = sources[:, :width], sources[:, width:]
        w = [tiles(factor, x * CHUNK, CHUNK, q) for q in range(LANE_TILES)]
        w_re, w_im = jnp.concatenate(w[:2], axis=1), jnp.concatenate(w[2:], axis=1)
        queries = jnp.concatenate([s_re * w_re - s_im * w_im, s_re * w_im + s_im * w_re], axis=1)
        q_high, q_low = high_low(queries)
        scores = dot(jnp.concatenate([q_high, q_high, q_low], axis=1), stack_t[1 - x])

        which = jnp.where(
            block_col == lax.broadcasted_iota(jnp.int32, (CHUNK, 2 * group), 1) % group, 1.0, 0.0
        ).astype(jnp.bfloat16)
        often = dot(which, times[x])

        small = jnp.exp(-jnp.abs(scores))
        near = 1.0 / (1.0 + small)
        far = small * near
        up = scores >= 0.0
        sig = jnp.where(up, near, far)
        sig_neg = jnp.where(up, far, near)
        g = sig * often - jnp.where(target_col == lane, sig_neg, 0.0)
        g = g * weight_col
        g_high, g_low = high_low(g)
        gq = dot(jnp.concatenate([g_high, g_high, g_low], axis=1), stack[1 - x])
        g_re, g_im = gq[:, :width], gq[:, width:]
        gw = [g_re * s_re + g_im * s_im, g_im * s_re - g_re * s_im]
        for q in range(LANE_TILES):
            flat = grads.reshape(2 * CHUNK * LANE_TILES, LANES)
            flat[pl.ds(x * CHUNK * LANE_TILES + q, CHUNK, stride=LANE_TILES), :] = gw[q // 2][
                :, (q % 2) * LANES : (q % 2 + 1) * LANES
            ]

        if x == 0:
            gs = jnp.concatenate([g_re * w_re + g_im * w_im, g_im * w_re - g_re * w_im], axis=1)
            sub = lax.broadcasted_iota(jnp.int32, (rows, CHUNK), 0)
            back = jnp.where(source_row - own == sub, 1.0, 0.0).astype(jnp.bfloat16)
            s_high, s_low = high_low(gs)
            mine[...] += dot(jnp.concatenate([back, back], axis=1), jnp.concatenate([s_high, s_low], axis=0))
        else:
            flip[...] = g.T
            turned = flip[pl.ds(pl.multiple_of(own, 8), rows), :]
            f_high, f_low = high_low(turned)
            mine[...] += dot(
                jnp.concatenate([f_high, f_high, f_low], axis=1),
                jnp.concatenate([q_high, q_low, q_high], axis=0),
            )

    def chunk(c, carry):
        start = c * CHUNK

        per = CHUNK // LANES
        row = c * per

        def fetch(k, carry):
            for x in range(2):
                for u in range(LANES):
                    factor[x * CHUNK + k * LANES + u] = table[ids[x, row + k, u]]
            return carry

        lax.fori_loop(0, per, fetch, 0)
        for x in range(2):
            compute(x, start)

        def push(k, carry):
            x = (k // per) ^ side
            k = k % per
            for e in range(0, LANES, 4):
                at = [ids[x, row + k, e + u] for u in range(4)]
                old = [accs[0][r] for r in at]
                for u in range(4):
                    value = old[u]
                    for v in range(u):
                        value = jnp.where(at[u] == at[v], old[v], value)
                    old[u] = value + grads[x * CHUNK + k * LANES + e + u]
                for u in range(4):
                    accs[0][at[u]] = old[u]
            return carry

        lax.fori_loop(0, 2 * per, push, 0)
        return carry

    lax.fori_loop(0, total // CHUNK, chunk, 0)

    ent_ref[:, :half] = mine[:, :half]
    ent_ref[:, half:] = mine[:, width : width + half]

    def finish(i, carry):
        at = pl.ds(pl.multiple_of(i * LANES, LANES), LANES)
        for q in range(LANE_TILES):
            sums = tiles(accs[0], i * LANES, LANES, q)
            for acc in accs[1:]:
                sums = sums + tiles(acc, i * LANES, LANES, q)
            low = (q // 2) * half + (q % 2) * LANES
            size = min(LANES, half - (q % 2) * LANES)
            out_ref[low : low + size, at] = sums.T[:size]
        return carry

    lax.fori_loop(0, relation_count // LANES, finish, 0)


def gradients(spec, sums, relation_count, *operands):
    half, rows, shards, blocks, edges = spec[:5]
    dim, part_rows, width = 2 * half, rows * shards, LANE_TILES // 2 * LANES
    group = shards * blocks
    total = group * edges // 2
    smem = pl.BlockSpec(memory_space=pltpu.SMEM)
    vmem = pl.BlockSpec(memory_space=pltpu.VMEM)
    return pl.pallas_call(
        functools.partial(main_kernel, spec),
        in_specs=[smem, smem, vmem, vmem, vmem, vmem],
        out_specs=(vmem, vmem),
        out_shape=(
            jax.ShapeDtypeStruct((dim, relation_count), jnp.float32),
            jax.ShapeDtypeStruct((rows, dim), jnp.float32),
        ),
        scratch_shapes=[pltpu.VMEM((relation_count, LANE_TILES, LANES), jnp.float32)] * sums
        + [
            pltpu.VMEM((part_rows, 2 * width), jnp.float32),
            pltpu.VMEM((2, 3 * part_rows, 2 * width), jnp.bfloat16),
            pltpu.VMEM((2, 6 * width, part_rows), jnp.bfloat16),
            pltpu.VMEM((2, 2 * group, part_rows), jnp.bfloat16),
            pltpu.VMEM((2, 8, total + edges + LANES), jnp.float32),
            pltpu.VMEM((2, total // LANES, LANES), jnp.int32),
            pltpu.SMEM((2, total // LANES, LANES), jnp.int32),
            pltpu.VMEM((2 * CHUNK, LANE_TILES, LANES), jnp.float32),
            pltpu.VMEM((2 * CHUNK, LANE_TILES, LANES), jnp.float32),
            pltpu.VMEM((part_rows, CHUNK), jnp.float32),
            pltpu.VMEM((rows, 2 * width), jnp.float32),
            pltpu.SemaphoreType.DMA,
        ],
        compiler_params=pltpu.CompilerParams(vmem_limit_bytes=VMEM_BYTES),
        name="gradients",
    )(*operands)


def body(entities, relations, src_index, dst_index, rel_index, neg_index, counts, edge_weight):
    rows, dim = entities.shape
    half = dim // 2
    width = LANE_TILES // 2 * LANES
    relation_count = relations.shape[0]
    blocks, edges = src_index.shape[1:]
    dom_count, shards = lax.axis_size("dom"), lax.axis_size("block")
    part_rows = rows * shards
    partner_bit = dom_count.bit_length() - 2
    block_bits = shards.bit_length() - 1
    other_bits = [bit for bit in range(dom_count.bit_length() - 1) if bit != partner_bit]

    table = relation_table(relations)

    real = jnp.pad(entities[:, :half], ((0, 0), (0, width - half)))
    imag = jnp.pad(entities[:, half:], ((0, 0), (0, width - half)))
    alive = jnp.arange(edges, dtype=jnp.int32)[None, :] < counts[0][:, None]
    weight = edge_weight[0] * alive.astype(jnp.float32)
    entity_ids = jnp.arange(part_rows, dtype=jnp.int32)
    times = jnp.sum((neg_index[0][:, :, None] == entity_ids).astype(jnp.float32), axis=1)
    times = times / neg_index.shape[2]
    ids = jnp.concatenate([src_index[0], dst_index[0], rel_index[0]], axis=0).astype(jnp.float32)
    info_a = jnp.concatenate([ids, weight], axis=0).reshape(-1, width)
    live_row = jnp.pad(counts[0].astype(jnp.float32)[None, :], ((0, 0), (0, width - blocks)))
    times_rows = blocks * part_rows // width
    info_b = jnp.concatenate([times.reshape(-1, width), live_row], axis=0)
    info_b = jnp.pad(info_b, ((0, -info_b.shape[0] % 8), (0, 0)))

    upper = [("block", bit) for bit in reversed(range(1, block_bits))]
    stages_a = upper + [("dom", partner_bit), ("block", 0)]
    stages_b = upper + [("block", 0), ("dom", partner_bit)]
    first = gather_all(jnp.concatenate([real, info_a], axis=0)[None], stages_a)
    second = gather_all(jnp.concatenate([imag, info_b], axis=0)[None], stages_b)
    places_a = tuple(stages_a.index(("block", bit)) for bit in range(block_bits))
    places_b = tuple(stages_b.index(("block", bit)) for bit in range(block_bits))
    place_a, place_b = stages_a.index(("dom", partner_bit)), stages_b.index(("dom", partner_bit))

    live = second[:, rows + times_rows, :blocks].astype(jnp.int32).reshape(-1)
    times_all = second[:, rows : rows + times_rows, :].reshape(-1, 1, part_rows)
    where = jnp.stack([lax.axis_index("block"), (lax.axis_index("dom") >> partner_bit) & 1]).astype(jnp.int32)

    sums = 1
    spec = (half, rows, shards, blocks, edges, places_a, places_b, place_a, place_b)
    relation_part, entity_grad = gradients(
        spec, sums, relation_count, live, where, table, first, second, times_all
    )

    for bit in other_bits:
        relation_part = relation_part + swap(relation_part, "dom", bit)
    return entity_grad, relation_part.T


def solution(mesh):
    placed = (
        P(("dom", "block"), None),
        P(),
        P("dom", "block", None),
        P("dom", "block", None),
        P("dom", "block", None),
        P("dom", "block", None),
        P("dom", "block"),
        P("dom", "block", None),
    )
    return jax.shard_map(
        body,
        mesh=mesh,
        in_specs=placed,
        out_specs=(P(("dom", "block"), None), P()),
        check_vma=False,
    )
```

```python
import functools

import jax
import jax.numpy as jnp
from jax import lax
from jax.experimental import pallas as pl
from jax.experimental.pallas import tpu as pltpu
from jax.sharding import PartitionSpec as P

LANES = 128
CHUNK = 256
GROUP = 8
STEP = 512
PARTS = 4
LANE_TILES = 4
SMALL_BYTES = 16 * 1024 * 1024


def swap(x, axis, bit):
    count = lax.axis_size(axis)
    return lax.ppermute(x, axis, [(i, i ^ (1 << bit)) for i in range(count)])


def gather_all(x, upper, lower):
    for axis, bit in upper:
        x = jnp.concatenate([x, swap(x, axis, bit)], axis=0)
    halves = list(jnp.split(x, 2))
    for k in range(2):
        others = [swap(halves[0], *lower[k]), swap(halves[1], *lower[1 - k])]
        halves = [jnp.concatenate(both, axis=0) for both in zip(halves, others)]
    return jnp.concatenate(halves, axis=0)


def block_index(j, x, bits):
    depth = bits - 1
    out = 0
    for stage in range(depth - 1):
        out = out | (((j >> (bits - 1 - stage)) & 1) << stage)
    half, low = (j >> 1) & 1, j & 1
    straight = (x << (depth - 1)) | (low << depth)
    crossed = (low << (depth - 1)) | (x << depth)
    return out | (half << (depth + 1)) | (straight + half * (crossed - straight))


def high_low(x):
    high = x.astype(jnp.bfloat16)
    return high, (x - high.astype(jnp.float32)).astype(jnp.bfloat16)


def dot(a, b):
    return jnp.dot(a, b, preferred_element_type=jnp.float32)


def pack_kernel(half, part_rows, counts, entities, src, dst, rel, neg, weight, out_ref):
    rows = entities.shape[0]
    blocks, edges = src.shape[1:]
    width = out_ref.shape[2]
    draws = neg.shape[2]
    base = rows + 4 * blocks
    gap = jnp.zeros((rows, width - half), jnp.float32)
    out = out_ref.at[0]
    out[:rows, :] = jnp.concatenate([entities[:, :half], gap], axis=1)
    out[base : base + rows, :] = jnp.concatenate([entities[:, half:], gap], axis=1)
    for k, ids in enumerate((src, dst, rel)):
        out[rows + k * blocks : rows + (k + 1) * blocks, :] = ids[0].astype(jnp.float32)
    slot = lax.broadcasted_iota(jnp.int32, (1, edges), 1)
    for i in range(blocks):
        row = rows + 3 * blocks + i
        out[row : row + 1, :] = jnp.where(slot < counts[0, i], weight[0, i : i + 1, :], 0.0)
    top = base + rows
    drawn = jnp.concatenate([neg[0], jnp.zeros((8 - blocks, draws), jnp.int32)], axis=0).astype(jnp.float32)
    drawn = drawn.T.astype(jnp.int32)
    lane = lax.broadcasted_iota(jnp.int32, (draws, part_rows), 1)
    for i in range(blocks):
        hits = jnp.where(drawn[:, i : i + 1] == lane, 1.0, 0.0).astype(jnp.bfloat16)
        times = dot(jnp.ones((8, draws), jnp.bfloat16), hits)[:1] / draws
        for part in range(part_rows // width):
            row = top + i * (part_rows // width) + part
            out[row : row + 1, :] = times[:, part * width : (part + 1) * width]
    top += blocks * (part_rows // width)
    spare = out_ref.shape[1] - top
    lane = lax.broadcasted_iota(jnp.int32, (spare, width), 1)
    last = jnp.zeros((spare, width), jnp.float32)
    for i in range(blocks):
        last = jnp.where(lane == i, counts[0, i].astype(jnp.float32), last)
    out[top:, :] = last


def packed(entities, counts, src, dst, rel, neg, weight, part_rows):
    rows, dim = entities.shape
    blocks = src.shape[1]
    width = LANE_TILES // 2 * LANES
    height = 2 * rows + 4 * blocks + blocks * (part_rows // width) + 1
    vmem = pl.BlockSpec(memory_space=pltpu.VMEM)
    return pl.pallas_call(
        functools.partial(pack_kernel, dim // 2, part_rows),
        in_specs=[pl.BlockSpec(memory_space=pltpu.SMEM)] + [vmem] * 6,
        out_specs=vmem,
        out_shape=jax.ShapeDtypeStruct((1, -(-height // 8) * 8, width), jnp.float32),
        compiler_params=pltpu.CompilerParams(vmem_limit_bytes=SMALL_BYTES),
        name="pack",
    )(counts, *[in_hbm(x) for x in (entities, src, dst, rel, neg, weight)])


def in_vmem(x):
    return pltpu.with_memory_space_constraint(x, pltpu.VMEM)


def in_hbm(x):
    return pltpu.with_memory_space_constraint(x, pltpu.HBM)


def finish_kernel(half, low, acc_ref, out_ref):
    for i in range(out_ref.shape[1] // LANES):
        for q in range(LANE_TILES):
            rows = tiles(acc_ref, low + i * LANES, LANES, q).T
            top = (q // 2) * half + (q % 2) * LANES
            size = min(LANES, half - (q % 2) * LANES)
            out_ref[top : top + size, i * LANES : (i + 1) * LANES] = rows[:size]


def add_kernel(one_ref, other_ref, *refs):
    refs[-1][...] = one_ref[...] + other_ref[...]


def summed(acc, dim, bits):
    count = acc.shape[0]
    size = count // PARTS
    parts = []
    for k in range(PARTS):
        part = pl.pallas_call(
            functools.partial(finish_kernel, dim // 2, k * size),
            in_specs=[pl.BlockSpec(memory_space=pltpu.VMEM)],
            out_specs=pl.BlockSpec(memory_space=pltpu.VMEM),
            out_shape=pltpu.VMEM((dim, size), jnp.float32),
            cost_estimate=pl.CostEstimate(flops=0, bytes_accessed=size * dim * 8, transcendentals=0),
            compiler_params=pltpu.CompilerParams(vmem_limit_bytes=SMALL_BYTES),
            name="turn",
        )(in_vmem(acc))
        for bit in bits[:-1]:
            part = part + swap(part, "dom", bit)
        parts.append((part, swap(part, "dom", bits[-1])))
    total = None
    for k, (part, other) in enumerate(parts):
        block = pl.BlockSpec((dim, size), lambda i: (0, 0))
        total = pl.pallas_call(
            add_kernel,
            grid=(1,),
            in_specs=[block, block] + ([] if total is None else [pl.BlockSpec(memory_space=pl.ANY)]),
            out_specs=pl.BlockSpec((dim, size), lambda i, k=k: (0, k)),
            out_shape=jax.ShapeDtypeStruct((dim, count), jnp.float32),
            input_output_aliases={} if total is None else {2: 0},
            cost_estimate=pl.CostEstimate(flops=size * dim, bytes_accessed=size * dim * 12, transcendentals=0),
            compiler_params=pltpu.CompilerParams(vmem_limit_bytes=SMALL_BYTES),
            name="add_part",
        )(part, other, *([] if total is None else [total]))
    return total


def tiles(ref, low, count, q):
    flat = ref.reshape(ref.shape[0] * ref.shape[1], LANES)
    return flat[pl.ds(low * LANE_TILES + q, count, stride=LANE_TILES), :]


STAGES = 5


def in_turn(parts, *sides):
    for stage in range(STAGES):
        for part in parts:
            next(part, None)
            for side, steps in sides:
                for _ in range(-(-steps // (STAGES * len(parts)))):
                    next(side, None)


def main_kernel(spec, live, where, relations, blocks_of, acc, ent_ref, *scratch):
    (half, rows, shards, blocks, edges) = spec
    (columns_of, table, ent, stack, stack_t, times, info, ids_v, ids, factor, grads, flip, mine, band, seg, come) = scratch
    width = LANE_TILES // 2 * LANES
    part_rows = rows * shards
    group = shards * blocks
    total = group * edges // 2
    bits = shards.bit_length() - 1
    base = rows + 4 * blocks
    top = base + rows
    me, side = where[0], where[1]
    own = me * rows

    steps = acc.shape[0] // STEP
    arrivals = []
    for k in range(steps):
        at = pl.ds(k * STEP, STEP)
        arrivals.append(pltpu.make_async_copy(relations.at[:, at], columns_of.at[:, at], come.at[k]))
        arrivals[-1].start()

    mine[...] = jnp.zeros_like(mine)
    info[...] = jnp.zeros_like(info)
    down = lax.broadcasted_iota(jnp.int32, band.shape, 0)
    across = lax.broadcasted_iota(jnp.int32, band.shape, 1)
    band[...] = jnp.where((across <= down) & (across // GROUP == down // GROUP), 1.0, 0.0)

    for x in range(2):
        for j in range(shards):
            k = block_index(j, x, bits)
            at = pl.ds(pl.multiple_of((j ^ me) * rows, 8), rows)
            ent[at, :width] = blocks_of[k, :rows, :]
            ent[at, width:] = blocks_of[k, base : base + rows, :]
        whole = ent[...]
        high, low = high_low(whole)
        stack[x] = jnp.concatenate([high, low, high], axis=0)
        high, low = high_low(whole.T)
        stack_t[x] = jnp.concatenate([high, low, high], axis=0)

    for x in range(2):
        rows_of = []
        for n in range(group):
            k = block_index((n // blocks) ^ me, x, bits)
            low = top + (n % blocks) * (part_rows // width)
            pieces = [blocks_of[k, low + i : low + i + 1, :] for i in range(part_rows // width)]
            rows_of.append(jnp.concatenate(pieces, axis=1))
        high, low = high_low(jnp.concatenate(rows_of, axis=0))
        times[x] = jnp.concatenate([high, low], axis=0)

        def lay(n, offset):
            k, slot = block_index((n // blocks) ^ me, x, bits), n % blocks
            count = live[k * blocks + slot]
            tile = blocks_of[k, rows : rows + 4 * blocks, :]

            def chosen(k):
                row = tile[k * blocks : k * blocks + 1]
                for i in range(1, blocks):
                    row = jnp.where(slot == i, tile[k * blocks + i : k * blocks + i + 1], row)
                return row

            number = jnp.zeros((1, edges), jnp.float32) + n.astype(jnp.float32)
            data = [chosen(k) for k in range(4)] + [number, jnp.zeros((3, edges), jnp.float32)]
            data = jnp.concatenate(data, axis=0)
            data = jnp.where(lax.broadcasted_iota(jnp.int32, data.shape, 1) < count, data, 0.0)
            data = jnp.concatenate([data, jnp.zeros((8, LANES), jnp.float32)], axis=1)
            data = pltpu.roll(data, offset % LANES, 1)
            at = pl.ds(pl.multiple_of((offset // LANES) * LANES, LANES), edges + LANES)
            info[x, :, at] = info[x, :, at] + data
            return offset + count

        lax.fori_loop(0, group, lay, jnp.int32(0))
        for i in range(total // LANES):
            ids_v[x, i : i + 1, :] = info[x, 2:3, i * LANES : (i + 1) * LANES].astype(jnp.int32)

    move = pltpu.make_async_copy(ids_v, ids, seg)
    move.start()

    def turn(k, carry):
        low = k * STEP
        at = pl.ds(pl.multiple_of(low, STEP), STEP)
        pltpu.make_async_copy(relations.at[:, at], columns_of.at[:, at], come.at[k]).wait()
        flat = table.reshape(table.shape[0] * LANE_TILES, LANES)
        for part in range(2):
            square = columns_of[part * half : (part + 1) * half, at]
            square = jnp.concatenate([square, jnp.zeros((width - half, STEP), jnp.float32)], axis=0).T
            for j in range(LANE_TILES // 2):
                to = pl.ds(low * LANE_TILES + part * (LANE_TILES // 2) + j, STEP, stride=LANE_TILES)
                flat[to, :] = square[:, j * LANES : (j + 1) * LANES]
        flat = acc.reshape(acc.shape[0] * LANE_TILES, LANES)
        to = pl.ds(pl.multiple_of(low * LANE_TILES, 8), STEP * LANE_TILES)
        flat[to, :] = jnp.zeros((STEP * LANE_TILES, LANES), jnp.float32)
        return carry

    lax.fori_loop(0, steps, turn, 0)
    move.wait()

    def row_id(x, at):
        return ids[x, at // LANES, at % LANES]

    def compute(x, start, slot):
        at = pl.ds(pl.multiple_of(start, CHUNK), CHUNK)
        data = info[x, :, at]
        columns = data.T
        source_row = data[0:1].astype(jnp.int32)
        source_col = columns[:, 0:1].astype(jnp.int32)
        target_col = columns[:, 1:2].astype(jnp.int32)
        weight_col = columns[:, 3:4]
        block_col = columns[:, 4:5].astype(jnp.int32)

        lane = lax.broadcasted_iota(jnp.int32, (CHUNK, part_rows), 1)
        pick = jnp.where(source_col == lane, 1.0, 0.0).astype(jnp.bfloat16)
        sources = dot(jnp.concatenate([pick, pick], axis=1), stack[x, : 2 * part_rows])
        yield
        s_re, s_im = sources[:, :width], sources[:, width:]
        w = [tiles(factor, (slot * 2 + x) * CHUNK, CHUNK, q) for q in range(LANE_TILES)]
        w_re, w_im = jnp.concatenate(w[:2], axis=1), jnp.concatenate(w[2:], axis=1)
        queries = jnp.concatenate([s_re * w_re - s_im * w_im, s_re * w_im + s_im * w_re], axis=1)
        q_high, q_low = high_low(queries)
        scores = dot(jnp.concatenate([q_high, q_high, q_low], axis=1), stack_t[1 - x])
        yield

        which = jnp.where(
            block_col == lax.broadcasted_iota(jnp.int32, (CHUNK, 2 * group), 1) % group, 1.0, 0.0
        ).astype(jnp.bfloat16)
        often = dot(which, times[x])

        small = jnp.exp(-jnp.abs(scores))
        near = 1.0 / (1.0 + small)
        far = small * near
        up = scores >= 0.0
        sig = jnp.where(up, near, far)
        sig_neg = jnp.where(up, far, near)
        g = sig * often - jnp.where(target_col == lane, sig_neg, 0.0)
        g = g * weight_col
        g_high, g_low = high_low(g)
        gq = dot(jnp.concatenate([g_high, g_high, g_low], axis=1), stack[1 - x])
        yield
        g_re, g_im = gq[:, :width], gq[:, width:]
        gw = jnp.concatenate([g_re * s_re + g_im * s_im, g_im * s_re - g_re * s_im], axis=1)
        same = jnp.where(columns[:, 2:3] == data[2:3], band[...], 0.0).astype(jnp.bfloat16)
        w_high, w_low = high_low(gw)
        gw = dot(jnp.concatenate([same, same], axis=1), jnp.concatenate([w_high, w_low], axis=0))
        yield
        flat = grads.reshape(4 * CHUNK * LANE_TILES, LANES)
        for q in range(LANE_TILES):
            at = pl.ds((slot * 2 + x) * CHUNK * LANE_TILES + q, CHUNK, stride=LANE_TILES)
            flat[at, :] = gw[:, q * LANES : (q + 1) * LANES]

        if x == 0:
            gs = jnp.concatenate([g_re * w_re + g_im * w_im, g_im * w_re - g_re * w_im], axis=1)
            sub = lax.broadcasted_iota(jnp.int32, (rows, CHUNK), 0)
            back = jnp.where(source_row - own == sub, 1.0, 0.0).astype(jnp.bfloat16)
            s_high, s_low = high_low(gs)
            mine[...] += dot(jnp.concatenate([back, back], axis=1), jnp.concatenate([s_high, s_low], axis=0))
        else:
            flip[...] = g.T
            turned = flip[pl.ds(pl.multiple_of(own, 8), rows), :]
            f_high, f_low = high_low(turned)
            mine[...] += dot(
                jnp.concatenate([f_high, f_high, f_low], axis=1),
                jnp.concatenate([q_high, q_low, q_high], axis=0),
            )

    per = CHUNK // LANES
    last = total // CHUNK - 1

    def fetch(c, slot):
        for e in range(0, CHUNK, 8):
            for x in range(2):
                for u in range(8):
                    row = table[ids[x, c * per + e // LANES, e % LANES + u]]
                    factor[(slot * 2 + x) * CHUNK + e + u] = row
            yield

    def push(c, slot):
        for turn in range(2):
            x = turn ^ side
            for e in range(0, CHUNK, GROUP):
                at = [ids[x, c * per + e // LANES, e % LANES + u] for u in range(GROUP)]
                new = [acc[r] + grads[(slot * 2 + x) * CHUNK + e + u] for u, r in enumerate(at)]
                for r, value in zip(at, new):
                    acc[r] = value
                yield

    def drain(steps):
        for _ in steps:
            pass

    def chunk(c, carry):
        slot = c & 1
        in_turn(
            [compute(x, c * CHUNK, slot) for x in range(2)],
            (fetch(jnp.minimum(c + 1, last), 1 - slot), CHUNK // 8),
            (push(jnp.maximum(c - 1, 0), 1 - slot), 2 * CHUNK // GROUP),
        )
        return carry

    def empty(i, carry):
        grads[pl.ds(2 * CHUNK + i * 8, 8)] = jnp.zeros((8, LANE_TILES, LANES), jnp.float32)
        return carry

    lax.fori_loop(0, 2 * CHUNK // 8, empty, 0)
    drain(fetch(0, 0))
    lax.fori_loop(0, last + 1, chunk, 0)
    drain(push(last, last % 2))

    ent_ref[:, :half] = mine[:, :half]
    ent_ref[:, half:] = mine[:, width : width + half]


def gradients(spec, relations, live, where, blocks_of):
    half, rows, shards, blocks, edges = spec
    dim, part_rows, width = 2 * half, rows * shards, LANE_TILES // 2 * LANES
    relation_count = relations.shape[0]
    group = shards * blocks
    total = group * edges // 2
    smem = pl.BlockSpec(memory_space=pltpu.SMEM)
    vmem = pl.BlockSpec(memory_space=pltpu.VMEM)
    return pl.pallas_call(
        functools.partial(main_kernel, spec),
        in_specs=[smem, smem, pl.BlockSpec(memory_space=pl.ANY), vmem],
        out_specs=(vmem, vmem),
        out_shape=(
            pltpu.VMEM((relation_count, LANE_TILES, LANES), jnp.float32),
            jax.ShapeDtypeStruct((rows, dim), jnp.float32),
        ),
        scratch_shapes=[
            pltpu.VMEM((dim, relation_count), jnp.float32),
            pltpu.VMEM((relation_count, LANE_TILES, LANES), jnp.float32),
            pltpu.VMEM((part_rows, 2 * width), jnp.float32),
            pltpu.VMEM((2, 3 * part_rows, 2 * width), jnp.bfloat16),
            pltpu.VMEM((2, 6 * width, part_rows), jnp.bfloat16),
            pltpu.VMEM((2, 2 * group, part_rows), jnp.bfloat16),
            pltpu.VMEM((2, 8, total + edges + LANES), jnp.float32),
            pltpu.VMEM((2, total // LANES, LANES), jnp.int32),
            pltpu.SMEM((2, total // LANES, LANES), jnp.int32),
            pltpu.VMEM((4 * CHUNK, LANE_TILES, LANES), jnp.float32),
            pltpu.VMEM((4 * CHUNK, LANE_TILES, LANES), jnp.float32),
            pltpu.VMEM((part_rows, CHUNK), jnp.float32),
            pltpu.VMEM((rows, 2 * width), jnp.float32),
            pltpu.VMEM((CHUNK, CHUNK), jnp.float32),
            pltpu.SemaphoreType.DMA,
            pltpu.SemaphoreType.DMA((relation_count // STEP,)),
        ],
        compiler_params=pltpu.CompilerParams(vmem_limit_bytes=(40 if part_rows <= 256 else 54) * 1024 * 1024),
        name="gradients",
    )(live, where, in_hbm(relations.T), blocks_of)


def body(entities, relations, src_index, dst_index, rel_index, neg_index, counts, edge_weight):
    rows, dim = entities.shape
    width = LANE_TILES // 2 * LANES
    blocks, edges = src_index.shape[1:]
    dom_count, shards = lax.axis_size("dom"), lax.axis_size("block")
    part_rows = rows * shards
    partner_bit = dom_count.bit_length() - 2
    block_bits = shards.bit_length() - 1
    other_bits = [bit for bit in range(dom_count.bit_length() - 1) if bit != partner_bit]

    block = packed(entities, counts, src_index, dst_index, rel_index, neg_index, edge_weight, part_rows)
    upper = [("block", bit) for bit in reversed(range(1, block_bits))]
    blocks_of = gather_all(block, upper, [("dom", partner_bit), ("block", 0)])
    last = 2 * rows + 4 * blocks + blocks * (part_rows // width)
    live = blocks_of[:, last, :blocks].astype(jnp.int32).reshape(-1)
    where = jnp.stack([lax.axis_index("block"), (lax.axis_index("dom") >> partner_bit) & 1]).astype(jnp.int32)

    spec = (dim // 2, rows, shards, blocks, edges)
    acc, entity_grad = gradients(spec, relations, live, where, blocks_of)
    return entity_grad, summed(acc, dim, other_bits).T


def solution(mesh):
    placed = (
        P(("dom", "block"), None),
        P(),
        P("dom", "block", None),
        P("dom", "block", None),
        P("dom", "block", None),
        P("dom", "block", None),
        P("dom", "block"),
        P("dom", "block", None),
    )
    return jax.shard_map(
        body,
        mesh=mesh,
        in_specs=placed,
        out_specs=(P(("dom", "block"), None), P()),
        check_vma=False,
    )
```

```python
import functools

import jax
import jax.numpy as jnp
from jax import lax
from jax.experimental import pallas as pl
from jax.experimental.pallas import tpu as pltpu
from jax.sharding import PartitionSpec as P

LANES = 128
CHUNK = 256
GROUP = 8
STEP = 512
PARTS = 4
LANE_TILES = 4
SMALL_BYTES = 16 * 1024 * 1024


def swap(x, axis, bit):
    count = lax.axis_size(axis)
    return lax.ppermute(x, axis, [(i, i ^ (1 << bit)) for i in range(count)])


def gather_all(x, upper, lower):
    for axis, bit in upper:
        x = jnp.concatenate([x, swap(x, axis, bit)], axis=0)
    halves = list(jnp.split(x, 2))
    for k in range(2):
        others = [swap(halves[0], *lower[k]), swap(halves[1], *lower[1 - k])]
        halves = [jnp.concatenate(both, axis=0) for both in zip(halves, others)]
    return jnp.concatenate(halves, axis=0)


def block_index(j, x, bits):
    depth = bits - 1
    out = 0
    for stage in range(depth - 1):
        out = out | (((j >> (bits - 1 - stage)) & 1) << stage)
    half, low = (j >> 1) & 1, j & 1
    straight = (x << (depth - 1)) | (low << depth)
    crossed = (low << (depth - 1)) | (x << depth)
    return out | (half << (depth + 1)) | (straight + half * (crossed - straight))


def high_low(x):
    high = x.astype(jnp.bfloat16)
    return high, (x - high.astype(jnp.float32)).astype(jnp.bfloat16)


def dot(a, b):
    return jnp.dot(a, b, preferred_element_type=jnp.float32)


def packing(half, rows, blocks, part_rows):
    width = LANE_TILES // 2 * LANES
    count = 4 * blocks + blocks * (part_rows // width) + 1
    room = width - half
    pieces = -(-width // room)
    return count, room, pieces, max(2 * rows, -(-pieces * count // 8) * 8)


def pack_kernel(half, part_rows, counts, entities, src, dst, rel, neg, weight, out_ref):
    rows = entities.shape[0]
    blocks, edges = src.shape[1:]
    width, height = out_ref.shape[2], out_ref.shape[1]
    draws = neg.shape[2]
    data = [ids[0].astype(jnp.float32) for ids in (src, dst, rel)]
    slot = lax.broadcasted_iota(jnp.int32, (1, edges), 1)
    for i in range(blocks):
        data.append(jnp.where(slot < counts[0, i], weight[0, i : i + 1, :], 0.0))
    drawn = jnp.concatenate([neg[0], jnp.zeros((8 - blocks, draws), jnp.int32)], axis=0).astype(jnp.float32)
    drawn = drawn.T.astype(jnp.int32)
    lane = lax.broadcasted_iota(jnp.int32, (draws, part_rows), 1)
    for i in range(blocks):
        hits = jnp.where(drawn[:, i : i + 1] == lane, 1.0, 0.0).astype(jnp.bfloat16)
        times = dot(jnp.ones((8, draws), jnp.bfloat16), hits)[:1] / draws
        data += [times[:, low : low + width] for low in range(0, part_rows, width)]
    last = jnp.zeros((1, width), jnp.float32)
    for i in range(blocks):
        last = jnp.where(slot == i, counts[0, i].astype(jnp.float32), last)
    data = jnp.concatenate(data + [last], axis=0)
    count, room, pieces, _ = packing(half, rows, blocks, part_rows)
    cut = [pltpu.roll(data, (half - room * piece) % width, 1) for piece in range(pieces)]
    cut.append(jnp.zeros((height - pieces * count, width), jnp.float32))
    beside = jnp.concatenate(cut, axis=0)
    gap = jnp.zeros((2 * rows, width - half), jnp.float32)
    held = jnp.concatenate([entities[:, :half], entities[:, half:]], axis=0)
    held = jnp.concatenate([held, gap], axis=1)
    if height > 2 * rows:
        held = jnp.concatenate([held, jnp.zeros((height - 2 * rows, width), jnp.float32)], axis=0)
    out_ref[0] = jnp.where(lax.broadcasted_iota(jnp.int32, held.shape, 1) < half, held, beside)


def packed(entities, counts, src, dst, rel, neg, weight, part_rows):
    rows, dim = entities.shape
    width = LANE_TILES // 2 * LANES
    height = packing(dim // 2, rows, src.shape[1], part_rows)[3]
    vmem = pl.BlockSpec(memory_space=pltpu.VMEM)
    return pl.pallas_call(
        functools.partial(pack_kernel, dim // 2, part_rows),
        in_specs=[pl.BlockSpec(memory_space=pltpu.SMEM)] + [vmem] * 6,
        out_specs=vmem,
        out_shape=jax.ShapeDtypeStruct((1, height, width), jnp.float32),
        compiler_params=pltpu.CompilerParams(vmem_limit_bytes=SMALL_BYTES),
        name="pack",
    )(counts, *[in_hbm(x) for x in (entities, src, dst, rel, neg, weight)])


def in_vmem(x):
    return pltpu.with_memory_space_constraint(x, pltpu.VMEM)


def in_hbm(x):
    return pltpu.with_memory_space_constraint(x, pltpu.HBM)


def finish_kernel(half, low, *refs):
    accs, out_ref = refs[:-1], refs[-1]
    for i in range(out_ref.shape[1] // LANES):
        for q in range(LANE_TILES):
            rows = sum(tiles(acc, low + i * LANES, LANES, q) for acc in accs).T
            top = (q // 2) * half + (q % 2) * LANES
            size = min(LANES, half - (q % 2) * LANES)
            out_ref[top : top + size, i * LANES : (i + 1) * LANES] = rows[:size]


def add_kernel(one_ref, other_ref, *refs):
    refs[-1][...] = one_ref[...] + other_ref[...]


def summed(accs, dim, bits):
    count = accs[0].shape[0]
    size = count // PARTS
    parts = []
    for k in range(PARTS):
        part = pl.pallas_call(
            functools.partial(finish_kernel, dim // 2, k * size),
            in_specs=[pl.BlockSpec(memory_space=pltpu.VMEM)] * len(accs),
            out_specs=pl.BlockSpec(memory_space=pltpu.VMEM),
            out_shape=pltpu.VMEM((dim, size), jnp.float32),
            cost_estimate=pl.CostEstimate(flops=0, bytes_accessed=size * dim * 8, transcendentals=0),
            compiler_params=pltpu.CompilerParams(vmem_limit_bytes=SMALL_BYTES),
            name="turn",
        )(*[in_vmem(acc) for acc in accs])
        for bit in bits[:-1]:
            part = part + swap(part, "dom", bit)
        parts.append((part, swap(part, "dom", bits[-1])))
    total = None
    for k, (part, other) in enumerate(parts):
        block = pl.BlockSpec((dim, size), lambda i: (0, 0))
        total = pl.pallas_call(
            add_kernel,
            grid=(1,),
            in_specs=[block, block] + ([] if total is None else [pl.BlockSpec(memory_space=pl.ANY)]),
            out_specs=pl.BlockSpec((dim, size), lambda i, k=k: (0, k)),
            out_shape=jax.ShapeDtypeStruct((dim, count), jnp.float32),
            input_output_aliases={} if total is None else {2: 0},
            cost_estimate=pl.CostEstimate(flops=size * dim, bytes_accessed=size * dim * 12, transcendentals=0),
            compiler_params=pltpu.CompilerParams(vmem_limit_bytes=SMALL_BYTES),
            name="add_part",
        )(part, other, *([] if total is None else [total]))
    return total


def tiles(ref, low, count, q):
    flat = ref.reshape(ref.shape[0] * ref.shape[1], LANES)
    return flat[pl.ds(low * LANE_TILES + q, count, stride=LANE_TILES), :]


STAGES = 4
SCRATCH = 16


def in_turn(parts, *sides):
    for stage in range(STAGES):
        for part in parts:
            next(part, None)
            for side, steps in sides:
                for _ in range(-(-steps // (STAGES * len(parts)))):
                    next(side, None)


def main_kernel(spec, live, where, relations, blocks_of, *refs):
    accs, ent_ref, scratch = refs[:-SCRATCH][:-1], refs[:-SCRATCH][-1], refs[-SCRATCH:]
    (half, rows, shards, blocks, edges) = spec
    (data_rows, columns_of, table, ent, stack, stack_t, times, info, ids_v, ids, factor, grads, flip, mine, seg, come) = scratch
    width = LANE_TILES // 2 * LANES
    part_rows = rows * shards
    group = shards * blocks
    total = group * edges // 2
    bits = shards.bit_length() - 1
    count, room, pieces, _ = packing(half, rows, blocks, part_rows)
    me, side = where[0], where[1]
    own = me * rows

    steps = accs[0].shape[0] // STEP
    arrivals = []
    for k in range(steps):
        at = pl.ds(k * STEP, STEP)
        arrivals.append(pltpu.make_async_copy(relations.at[:, at], columns_of.at[:, at], come.at[k]))
        arrivals[-1].start()

    mine[...] = jnp.zeros_like(mine)
    info[...] = jnp.zeros_like(info)

    for x in range(2):
        for j in range(shards):
            k = block_index(j, x, bits)
            at = pl.ds(pl.multiple_of((j ^ me) * rows, 8), rows)
            lane = lax.broadcasted_iota(jnp.int32, (rows, width), 1)
            for part in range(2):
                square = blocks_of[k, part * rows : (part + 1) * rows, :]
                ent[at, part * width : (part + 1) * width] = jnp.where(lane < half, square, 0.0)
            lane = lax.broadcasted_iota(jnp.int32, (count, width), 1)
            raw = jnp.zeros((count, width), jnp.float32)
            for piece in range(pieces):
                square = pltpu.roll(
                    blocks_of[k, piece * count : (piece + 1) * count, :], (room * piece - half) % width, 1
                )
                raw = jnp.where((lane >= room * piece) & (lane < room * (piece + 1)), square, raw)
            data_rows[k, :count, :] = raw
        whole = ent[...]
        high, low = high_low(whole)
        stack[x] = jnp.concatenate([high, low, high], axis=0)
        high, low = high_low(whole.T)
        stack_t[x] = jnp.concatenate([high, low, high], axis=0)

    for x in range(2):
        rows_of = []
        for n in range(group):
            k = block_index((n // blocks) ^ me, x, bits)
            low = 4 * blocks + (n % blocks) * (part_rows // width)
            whole = [data_rows[k, low + i : low + i + 1, :] for i in range(part_rows // width)]
            rows_of.append(jnp.concatenate(whole, axis=1))
        high, low = high_low(jnp.concatenate(rows_of, axis=0))
        times[x] = jnp.concatenate([high, low], axis=0)

        def lay(n, offset):
            k, slot = block_index((n // blocks) ^ me, x, bits), n % blocks
            alive = live[k * blocks + slot]
            tile = data_rows[k, : 4 * blocks, :]

            def chosen(k):
                row = tile[k * blocks : k * blocks + 1]
                for i in range(1, blocks):
                    row = jnp.where(slot == i, tile[k * blocks + i : k * blocks + i + 1], row)
                return row

            number = jnp.zeros((1, edges), jnp.float32) + n.astype(jnp.float32)
            data = [chosen(k) for k in range(4)] + [number, jnp.zeros((3, edges), jnp.float32)]
            data = jnp.concatenate(data, axis=0)
            data = jnp.where(lax.broadcasted_iota(jnp.int32, data.shape, 1) < alive, data, 0.0)
            data = jnp.concatenate([data, jnp.zeros((8, LANES), jnp.float32)], axis=1)
            data = pltpu.roll(data, offset % LANES, 1)
            at = pl.ds(pl.multiple_of((offset // LANES) * LANES, LANES), edges + LANES)
            info[x, :, at] = info[x, :, at] + data
            return offset + alive

        lax.fori_loop(0, group, lay, jnp.int32(0))
        for i in range(total // LANES):
            ids_v[x, i : i + 1, :] = info[x, 2:3, i * LANES : (i + 1) * LANES].astype(jnp.int32)

    move = pltpu.make_async_copy(ids_v, ids, seg)
    move.start()

    def turn(k, carry):
        low = k * STEP
        at = pl.ds(pl.multiple_of(low, STEP), STEP)
        pltpu.make_async_copy(relations.at[:, at], columns_of.at[:, at], come.at[k]).wait()
        flat = table.reshape(table.shape[0] * LANE_TILES, LANES)
        for part in range(2):
            square = columns_of[part * half : (part + 1) * half, at]
            square = jnp.concatenate([square, jnp.zeros((width - half, STEP), jnp.float32)], axis=0).T
            for j in range(LANE_TILES // 2):
                to = pl.ds(low * LANE_TILES + part * (LANE_TILES // 2) + j, STEP, stride=LANE_TILES)
                flat[to, :] = square[:, j * LANES : (j + 1) * LANES]
        to = pl.ds(pl.multiple_of(low * LANE_TILES, 8), STEP * LANE_TILES)
        for acc in accs:
            flat = acc.reshape(acc.shape[0] * LANE_TILES, LANES)
            flat[to, :] = jnp.zeros((STEP * LANE_TILES, LANES), jnp.float32)
        return carry

    lax.fori_loop(0, steps, turn, 0)
    move.wait()

    def row_id(x, at):
        return ids[x, at // LANES, at % LANES]

    def compute(x, start, slot):
        at = pl.ds(pl.multiple_of(start, CHUNK), CHUNK)
        data = info[x, :, at]
        columns = data.T
        source_row = data[0:1].astype(jnp.int32)
        source_col = columns[:, 0:1].astype(jnp.int32)
        target_col = columns[:, 1:2].astype(jnp.int32)
        weight_col = columns[:, 3:4]
        block_col = columns[:, 4:5].astype(jnp.int32)

        lane = lax.broadcasted_iota(jnp.int32, (CHUNK, part_rows), 1)
        pick = jnp.where(source_col == lane, 1.0, 0.0).astype(jnp.bfloat16)
        sources = dot(jnp.concatenate([pick, pick], axis=1), stack[x, : 2 * part_rows])
        yield
        s_re, s_im = sources[:, :width], sources[:, width:]
        w = [tiles(factor, (slot * 2 + x) * CHUNK, CHUNK, q) for q in range(LANE_TILES)]
        w_re, w_im = jnp.concatenate(w[:2], axis=1), jnp.concatenate(w[2:], axis=1)
        queries = jnp.concatenate([s_re * w_re - s_im * w_im, s_re * w_im + s_im * w_re], axis=1)
        q_high, q_low = high_low(queries)
        scores = dot(jnp.concatenate([q_high, q_high, q_low], axis=1), stack_t[1 - x])
        yield

        which = jnp.where(
            block_col == lax.broadcasted_iota(jnp.int32, (CHUNK, 2 * group), 1) % group, 1.0, 0.0
        ).astype(jnp.bfloat16)
        often = dot(which, times[x])

        sig = 1.0 / (1.0 + jnp.exp(-scores))
        sig_neg = 1.0 / (1.0 + jnp.exp(scores))
        g = sig * often - jnp.where(target_col == lane, sig_neg, 0.0)
        g = g * weight_col
        g_high, g_low = high_low(g)
        gq = dot(jnp.concatenate([g_high, g_high, g_low], axis=1), stack[1 - x])
        yield
        g_re, g_im = gq[:, :width], gq[:, width:]
        gw = jnp.concatenate([g_re * s_re + g_im * s_im, g_im * s_re - g_re * s_im], axis=1)
        flat = grads.reshape(4 * CHUNK * LANE_TILES, LANES)
        for q in range(LANE_TILES):
            at = pl.ds((slot * 2 + x) * CHUNK * LANE_TILES + q, CHUNK, stride=LANE_TILES)
            flat[at, :] = gw[:, q * LANES : (q + 1) * LANES]

        if x == 0:
            gs = jnp.concatenate([g_re * w_re + g_im * w_im, g_im * w_re - g_re * w_im], axis=1)
            sub = lax.broadcasted_iota(jnp.int32, (rows, CHUNK), 0)
            back = jnp.where(source_row - own == sub, 1.0, 0.0).astype(jnp.bfloat16)
            s_high, s_low = high_low(gs)
            mine[...] += dot(jnp.concatenate([back, back], axis=1), jnp.concatenate([s_high, s_low], axis=0))
        else:
            flip[...] = g.T
            turned = flip[pl.ds(pl.multiple_of(own, 8), rows), :]
            f_high, f_low = high_low(turned)
            mine[...] += dot(
                jnp.concatenate([f_high, f_high, f_low], axis=1),
                jnp.concatenate([q_high, q_low, q_high], axis=0),
            )

    per = CHUNK // LANES
    last = total // CHUNK - 1

    def fetch(c, slot):
        for e in range(0, CHUNK, 8):
            for x in range(2):
                for u in range(8):
                    row = table[ids[x, c * per + e // LANES, e % LANES + u]]
                    factor[(slot * 2 + x) * CHUNK + e + u] = row
            yield

    def push(c, slot):
        for e in range(0, CHUNK, GROUP):
            for u in range(GROUP):
                for order in range(2):
                    acc = accs[order % len(accs)]
                    x = order ^ side
                    r = ids[x, c * per + e // LANES, e % LANES + u]
                    acc[r] = acc[r] + grads[(slot * 2 + x) * CHUNK + e + u]
            yield

    def drain(steps):
        for _ in steps:
            pass

    def chunk(c, carry):
        slot = c & 1
        in_turn(
            [compute(x, c * CHUNK, slot) for x in range(2)],
            (fetch(jnp.minimum(c + 1, last), 1 - slot), CHUNK // 8),
            (push(jnp.maximum(c - 1, 0), 1 - slot), CHUNK // GROUP),
        )
        return carry

    def empty(i, carry):
        grads[pl.ds(2 * CHUNK + i * 8, 8)] = jnp.zeros((8, LANE_TILES, LANES), jnp.float32)
        return carry

    lax.fori_loop(0, 2 * CHUNK // 8, empty, 0)
    drain(fetch(0, 0))
    lax.fori_loop(0, last + 1, chunk, 0)
    drain(push(last, last % 2))

    ent_ref[:, :half] = mine[:, :half]
    ent_ref[:, half:] = mine[:, width : width + half]


def gradients(spec, relations, live, where, blocks_of):
    half, rows, shards, blocks, edges = spec
    dim, part_rows, width = 2 * half, rows * shards, LANE_TILES // 2 * LANES
    relation_count = relations.shape[0]
    group = shards * blocks
    total = group * edges // 2
    totals = 2 if part_rows <= 256 else 1
    smem = pl.BlockSpec(memory_space=pltpu.SMEM)
    vmem = pl.BlockSpec(memory_space=pltpu.VMEM)
    return pl.pallas_call(
        functools.partial(main_kernel, spec),
        in_specs=[smem, smem, pl.BlockSpec(memory_space=pl.ANY), vmem],
        out_specs=(vmem,) * (totals + 1),
        out_shape=(
            *[pltpu.VMEM((relation_count, LANE_TILES, LANES), jnp.float32)] * totals,
            jax.ShapeDtypeStruct((rows, dim), jnp.float32),
        ),
        scratch_shapes=[
            pltpu.VMEM((2 * shards, -(-packing(half, rows, blocks, part_rows)[0] // 8) * 8, width), jnp.float32),
            pltpu.VMEM((dim, relation_count), jnp.float32),
            pltpu.VMEM((relation_count, LANE_TILES, LANES), jnp.float32),
            pltpu.VMEM((part_rows, 2 * width), jnp.float32),
            pltpu.VMEM((2, 3 * part_rows, 2 * width), jnp.bfloat16),
            pltpu.VMEM((2, 6 * width, part_rows), jnp.bfloat16),
            pltpu.VMEM((2, 2 * group, part_rows), jnp.bfloat16),
            pltpu.VMEM((2, 8, total + edges + LANES), jnp.float32),
            pltpu.VMEM((2, total // LANES, LANES), jnp.int32),
            pltpu.SMEM((2, total // LANES, LANES), jnp.int32),
            pltpu.VMEM((4 * CHUNK, LANE_TILES, LANES), jnp.float32),
            pltpu.VMEM((4 * CHUNK, LANE_TILES, LANES), jnp.float32),
            pltpu.VMEM((part_rows, CHUNK), jnp.float32),
            pltpu.VMEM((rows, 2 * width), jnp.float32),
            pltpu.SemaphoreType.DMA,
            pltpu.SemaphoreType.DMA((relation_count // STEP,)),
        ],
        compiler_params=pltpu.CompilerParams(vmem_limit_bytes=(40 if part_rows <= 256 else 54) * 1024 * 1024),
        name="gradients",
    )(live, where, in_hbm(relations.T), blocks_of)


def body(entities, relations, src_index, dst_index, rel_index, neg_index, counts, edge_weight):
    rows, dim = entities.shape
    blocks, edges = src_index.shape[1:]
    dom_count, shards = lax.axis_size("dom"), lax.axis_size("block")
    part_rows = rows * shards
    partner_bit = dom_count.bit_length() - 2
    block_bits = shards.bit_length() - 1
    other_bits = [bit for bit in range(dom_count.bit_length() - 1) if bit != partner_bit]

    block = packed(entities, counts, src_index, dst_index, rel_index, neg_index, edge_weight, part_rows)
    upper = [("block", bit) for bit in reversed(range(1, block_bits))]
    blocks_of = gather_all(block, upper, [("dom", partner_bit), ("block", 0)])
    last = packing(dim // 2, rows, blocks, part_rows)[0] - 1
    live = blocks_of[:, last, dim // 2 : dim // 2 + blocks].astype(jnp.int32).reshape(-1)
    where = jnp.stack([lax.axis_index("block"), (lax.axis_index("dom") >> partner_bit) & 1]).astype(jnp.int32)

    spec = (dim // 2, rows, shards, blocks, edges)
    *accs, entity_grad = gradients(spec, relations, live, where, blocks_of)
    return entity_grad, summed(accs, dim, other_bits).T


def solution(mesh):
    placed = (
        P(("dom", "block"), None),
        P(),
        P("dom", "block", None),
        P("dom", "block", None),
        P("dom", "block", None),
        P("dom", "block", None),
        P("dom", "block"),
        P("dom", "block", None),
    )
    return jax.shard_map(
        body,
        mesh=mesh,
        in_specs=placed,
        out_specs=(P(("dom", "block"), None), P()),
        check_vma=False,
    )
```

```python
import functools

import jax
import jax.numpy as jnp
from jax import lax
from jax.experimental import pallas as pl
from jax.experimental.pallas import tpu as pltpu
from jax.sharding import PartitionSpec as P

LANES = 128
CHUNK = 256
GROUP = 8
STEP = 512
PARTS = 4
LANE_TILES = 4
SMALL_BYTES = 16 * 1024 * 1024


def swap(x, axis, bit):
    count = lax.axis_size(axis)
    return lax.ppermute(x, axis, [(i, i ^ (1 << bit)) for i in range(count)])


def gather_all(x, upper, lower):
    while upper:
        stage, upper = upper[:2], upper[2:]
        others = [swap(x, *step) for step in stage]
        if len(stage) == 2:
            (axis, bit), (_, other) = stage
            count = lax.axis_size(axis)
            others.append(lax.ppermute(x, axis, [(i, i ^ (1 << bit) ^ (1 << other)) for i in range(count)]))
        x = jnp.concatenate([x] + others, axis=0)
    halves = list(jnp.split(x, 2))
    for k in range(2):
        others = [swap(halves[0], *lower[k]), swap(halves[1], *lower[1 - k])]
        halves = [jnp.concatenate(both, axis=0) for both in zip(halves, others)]
    return jnp.concatenate(halves, axis=0)


def block_index(j, x, bits):
    depth = bits - 1
    out = 0
    for stage in range(depth - 1):
        out = out | (((j >> (bits - 1 - stage)) & 1) << stage)
    half, low = (j >> 1) & 1, j & 1
    straight = (x << (depth - 1)) | (low << depth)
    crossed = (low << (depth - 1)) | (x << depth)
    return out | (half << (depth + 1)) | (straight + half * (crossed - straight))


def high_low(x):
    high = x.astype(jnp.bfloat16)
    return high, (x - high.astype(jnp.float32)).astype(jnp.bfloat16)


def dot(a, b):
    return jnp.dot(a, b, preferred_element_type=jnp.float32)


def packing(half, rows, blocks, part_rows):
    width = LANE_TILES // 2 * LANES
    count = 4 * blocks + blocks * (part_rows // width) + 1
    room = width - half
    pieces = -(-width // room)
    return count, room, pieces, max(2 * rows, -(-pieces * count // 8) * 8)


def pack_kernel(half, part_rows, counts, entities, src, dst, rel, neg, weight, out_ref):
    rows = entities.shape[0]
    blocks, edges = src.shape[1:]
    width, height = out_ref.shape[2], out_ref.shape[1]
    draws = neg.shape[2]
    data = [ids[0].astype(jnp.float32) for ids in (src, dst, rel)]
    slot = lax.broadcasted_iota(jnp.int32, (1, edges), 1)
    for i in range(blocks):
        data.append(jnp.where(slot < counts[0, i], weight[0, i : i + 1, :], 0.0))
    drawn = jnp.concatenate([neg[0], jnp.zeros((8 - blocks, draws), jnp.int32)], axis=0).astype(jnp.float32)
    drawn = drawn.T.astype(jnp.int32)
    lane = lax.broadcasted_iota(jnp.int32, (draws, part_rows), 1)
    for i in range(blocks):
        hits = jnp.where(drawn[:, i : i + 1] == lane, 1.0, 0.0).astype(jnp.bfloat16)
        times = dot(jnp.ones((8, draws), jnp.bfloat16), hits)[:1] / draws
        data += [times[:, low : low + width] for low in range(0, part_rows, width)]
    last = jnp.zeros((1, width), jnp.float32)
    for i in range(blocks):
        last = jnp.where(slot == i, counts[0, i].astype(jnp.float32), last)
    data = jnp.concatenate(data + [last], axis=0)
    count, room, pieces, _ = packing(half, rows, blocks, part_rows)
    cut = [pltpu.roll(data, (half - room * piece) % width, 1) for piece in range(pieces)]
    cut.append(jnp.zeros((height - pieces * count, width), jnp.float32))
    beside = jnp.concatenate(cut, axis=0)
    gap = jnp.zeros((2 * rows, width - half), jnp.float32)
    held = jnp.concatenate([entities[:, :half], entities[:, half:]], axis=0)
    held = jnp.concatenate([held, gap], axis=1)
    if height > 2 * rows:
        held = jnp.concatenate([held, jnp.zeros((height - 2 * rows, width), jnp.float32)], axis=0)
    out_ref[0] = jnp.where(lax.broadcasted_iota(jnp.int32, held.shape, 1) < half, held, beside)


def packed(entities, counts, src, dst, rel, neg, weight, part_rows):
    rows, dim = entities.shape
    width = LANE_TILES // 2 * LANES
    height = packing(dim // 2, rows, src.shape[1], part_rows)[3]
    vmem = pl.BlockSpec(memory_space=pltpu.VMEM)
    return pl.pallas_call(
        functools.partial(pack_kernel, dim // 2, part_rows),
        in_specs=[pl.BlockSpec(memory_space=pltpu.SMEM)] + [vmem] * 6,
        out_specs=vmem,
        out_shape=jax.ShapeDtypeStruct((1, height, width), jnp.float32),
        compiler_params=pltpu.CompilerParams(vmem_limit_bytes=SMALL_BYTES),
        name="pack",
    )(*[in_hbm(x) for x in (counts, entities, src, dst, rel, neg, weight)])


def in_vmem(x):
    return pltpu.with_memory_space_constraint(x, pltpu.VMEM)


def in_hbm(x):
    return pltpu.with_memory_space_constraint(x, pltpu.HBM)


def finish_kernel(half, low, *refs):
    accs, out_ref = refs[:-1], refs[-1]
    for i in range(out_ref.shape[1] // LANES):
        for q in range(LANE_TILES):
            rows = sum(tiles(acc, low + i * LANES, LANES, q) for acc in accs).T
            top = (q // 2) * half + (q % 2) * LANES
            size = min(LANES, half - (q % 2) * LANES)
            out_ref[top : top + size, i * LANES : (i + 1) * LANES] = rows[:size]


def add_kernel(one_ref, other_ref, *refs):
    refs[-1][...] = one_ref[...] + other_ref[...]


def summed(accs, dim, bits):
    count = accs[0].shape[0]
    size = count // PARTS
    parts = []
    for k in range(PARTS):
        part = pl.pallas_call(
            functools.partial(finish_kernel, dim // 2, k * size),
            in_specs=[pl.BlockSpec(memory_space=pltpu.VMEM)] * len(accs),
            out_specs=pl.BlockSpec(memory_space=pltpu.VMEM),
            out_shape=pltpu.VMEM((dim, size), jnp.float32),
            cost_estimate=pl.CostEstimate(flops=0, bytes_accessed=size * dim * 8, transcendentals=0),
            compiler_params=pltpu.CompilerParams(vmem_limit_bytes=SMALL_BYTES),
            name="turn",
        )(*[in_vmem(acc) for acc in accs])
        for bit in bits[:-1]:
            part = part + swap(part, "dom", bit)
        parts.append((part, swap(part, "dom", bits[-1])))
    total = None
    for k, (part, other) in enumerate(parts):
        block = pl.BlockSpec((dim, size), lambda i: (0, 0))
        total = pl.pallas_call(
            add_kernel,
            grid=(1,),
            in_specs=[block, block] + ([] if total is None else [pl.BlockSpec(memory_space=pl.ANY)]),
            out_specs=pl.BlockSpec((dim, size), lambda i, k=k: (0, k)),
            out_shape=jax.ShapeDtypeStruct((dim, count), jnp.float32),
            input_output_aliases={} if total is None else {2: 0},
            cost_estimate=pl.CostEstimate(flops=size * dim, bytes_accessed=size * dim * 12, transcendentals=0),
            compiler_params=pltpu.CompilerParams(vmem_limit_bytes=SMALL_BYTES),
            name="add_part",
        )(part, other, *([] if total is None else [total]))
    return total


def tiles(ref, low, count, q):
    flat = ref.reshape(ref.shape[0] * ref.shape[1], LANES)
    return flat[pl.ds(low * LANE_TILES + q, count, stride=LANE_TILES), :]


STAGES = 4
FIRST = 2
SCRATCH = 19


def in_turn(parts, *sides):
    for stage in range(STAGES):
        for part in parts:
            next(part, None)
            for side, steps in sides if stage >= FIRST else []:
                for _ in range(-(-steps // ((STAGES - FIRST) * len(parts)))):
                    next(side, None)


def main_kernel(spec, where, relations, blocks_of, *refs):
    accs, ent_ref, scratch = refs[:-SCRATCH][:-1], refs[:-SCRATCH][-1], refs[-SCRATCH:]
    (half, rows, shards, blocks, edges) = spec
    (live_v, live, data_rows, columns_of, table, ent, stack, stack_t, times, info, ids_v, ids, factor, grads, flip, mine, seg, come, known) = scratch
    width = LANE_TILES // 2 * LANES
    part_rows = rows * shards
    group = shards * blocks
    total = group * edges // 2
    bits = shards.bit_length() - 1
    count, room, pieces, _ = packing(half, rows, blocks, part_rows)
    me, side = where[0], where[1]
    own = me * rows

    steps = accs[0].shape[0] // STEP
    arrivals = []
    for k in range(steps):
        at = pl.ds(k * STEP, STEP)
        arrivals.append(pltpu.make_async_copy(relations.at[:, at], columns_of.at[:, at], come.at[k]))
        arrivals[-1].start()

    mine[...] = jnp.zeros_like(mine)
    info[...] = jnp.zeros_like(info)

    lane = lax.broadcasted_iota(jnp.int32, (count, width), 1)
    for k in range(2 * shards):
        raw = jnp.zeros((count, width), jnp.float32)
        for piece in range(pieces):
            square = blocks_of[k, piece * count : (piece + 1) * count, :]
            square = pltpu.roll(square, (room * piece - half) % width, 1)
            raw = jnp.where((lane >= room * piece) & (lane < room * (piece + 1)), square, raw)
        data_rows[k, :count, :] = raw
        live_v[k : k + 1, :] = raw[count - 1 :, :LANES].astype(jnp.int32)
    tell = pltpu.make_async_copy(live_v, live, known)
    tell.start()

    for x in range(2):
        for j in range(shards):
            k = block_index(j, x, bits)
            at = pl.ds(pl.multiple_of((j ^ me) * rows, 8), rows)
            lane = lax.broadcasted_iota(jnp.int32, (rows, width), 1)
            for part in range(2):
                square = blocks_of[k, part * rows : (part + 1) * rows, :]
                ent[at, part * width : (part + 1) * width] = jnp.where(lane < half, square, 0.0)
        whole = ent[...]
        high, low = high_low(whole)
        stack[x] = jnp.concatenate([high, low, high], axis=0)
        high, low = high_low(whole.T)
        stack_t[x] = jnp.concatenate([high, low, high], axis=0)

    tell.wait()

    for x in range(2):
        rows_of = []
        for n in range(group):
            k = block_index((n // blocks) ^ me, x, bits)
            low = 4 * blocks + (n % blocks) * (part_rows // width)
            whole = [data_rows[k, low + i : low + i + 1, :] for i in range(part_rows // width)]
            rows_of.append(jnp.concatenate(whole, axis=1))
        high, low = high_low(jnp.concatenate(rows_of, axis=0))
        times[x] = jnp.concatenate([high, low], axis=0)

        def lay(n, offset):
            k, slot = block_index((n // blocks) ^ me, x, bits), n % blocks
            alive = live[k, slot]
            tile = data_rows[k, : 4 * blocks, :]

            def chosen(k):
                row = tile[k * blocks : k * blocks + 1]
                for i in range(1, blocks):
                    row = jnp.where(slot == i, tile[k * blocks + i : k * blocks + i + 1], row)
                return row

            number = jnp.zeros((1, edges), jnp.float32) + n.astype(jnp.float32)
            data = [chosen(k) for k in range(4)] + [number, jnp.zeros((3, edges), jnp.float32)]
            data = jnp.concatenate(data, axis=0)
            data = jnp.where(lax.broadcasted_iota(jnp.int32, data.shape, 1) < alive, data, 0.0)
            data = jnp.concatenate([data, jnp.zeros((8, LANES), jnp.float32)], axis=1)
            data = pltpu.roll(data, offset % LANES, 1)
            at = pl.ds(pl.multiple_of((offset // LANES) * LANES, LANES), edges + LANES)
            info[x, :, at] = info[x, :, at] + data
            return offset + alive

        lax.fori_loop(0, group, lay, jnp.int32(0))
        for i in range(total // LANES):
            ids_v[x, i : i + 1, :] = info[x, 2:3, i * LANES : (i + 1) * LANES].astype(jnp.int32)

    move = pltpu.make_async_copy(ids_v, ids, seg)
    move.start()

    def turn(k, carry):
        low = k * STEP
        at = pl.ds(pl.multiple_of(low, STEP), STEP)
        pltpu.make_async_copy(relations.at[:, at], columns_of.at[:, at], come.at[k]).wait()
        flat = table.reshape(table.shape[0] * LANE_TILES, LANES)
        for part in range(2):
            square = columns_of[part * half : (part + 1) * half, at]
            square = jnp.concatenate([square, jnp.zeros((width - half, STEP), jnp.float32)], axis=0).T
            for j in range(LANE_TILES // 2):
                to = pl.ds(low * LANE_TILES + part * (LANE_TILES // 2) + j, STEP, stride=LANE_TILES)
                flat[to, :] = square[:, j * LANES : (j + 1) * LANES]
        to = pl.ds(pl.multiple_of(low * LANE_TILES, 8), STEP * LANE_TILES)
        for acc in accs:
            flat = acc.reshape(acc.shape[0] * LANE_TILES, LANES)
            flat[to, :] = jnp.zeros((STEP * LANE_TILES, LANES), jnp.float32)
        return carry

    lax.fori_loop(0, steps, turn, 0)
    move.wait()

    def row_id(x, at):
        return ids[x, at // LANES, at % LANES]

    def compute(x, start, slot):
        at = pl.ds(pl.multiple_of(start, CHUNK), CHUNK)
        data = info[x, :, at]
        columns = data.T
        source_row = data[0:1].astype(jnp.int32)
        source_col = columns[:, 0:1].astype(jnp.int32)
        target_col = columns[:, 1:2].astype(jnp.int32)
        weight_col = columns[:, 3:4]
        block_col = columns[:, 4:5].astype(jnp.int32)

        lane = lax.broadcasted_iota(jnp.int32, (CHUNK, part_rows), 1)
        pick = jnp.where(source_col == lane, 1.0, 0.0).astype(jnp.bfloat16)
        sources = dot(jnp.concatenate([pick, pick], axis=1), stack[x, : 2 * part_rows])
        yield
        s_re, s_im = sources[:, :width], sources[:, width:]
        w = [tiles(factor, (slot * 2 + x) * CHUNK, CHUNK, q) for q in range(LANE_TILES)]
        w_re, w_im = jnp.concatenate(w[:2], axis=1), jnp.concatenate(w[2:], axis=1)
        queries = jnp.concatenate([s_re * w_re - s_im * w_im, s_re * w_im + s_im * w_re], axis=1)
        q_high, q_low = high_low(queries)
        scores = dot(jnp.concatenate([q_high, q_high, q_low], axis=1), stack_t[1 - x])
        yield

        which = jnp.where(
            block_col == lax.broadcasted_iota(jnp.int32, (CHUNK, 2 * group), 1) % group, 1.0, 0.0
        ).astype(jnp.bfloat16)
        often = dot(which, times[x])

        sig = 1.0 / (1.0 + jnp.exp(-scores))
        sig_neg = 1.0 / (1.0 + jnp.exp(scores))
        g = sig * often - jnp.where(target_col == lane, sig_neg, 0.0)
        g = g * weight_col
        g_high, g_low = high_low(g)
        gq = dot(jnp.concatenate([g_high, g_high, g_low], axis=1), stack[1 - x])
        yield
        g_re, g_im = gq[:, :width], gq[:, width:]
        gw = jnp.concatenate([g_re * s_re + g_im * s_im, g_im * s_re - g_re * s_im], axis=1)
        flat = grads.reshape(4 * CHUNK * LANE_TILES, LANES)
        for q in range(LANE_TILES):
            at = pl.ds((slot * 2 + x) * CHUNK * LANE_TILES + q, CHUNK, stride=LANE_TILES)
            flat[at, :] = gw[:, q * LANES : (q + 1) * LANES]

        if x == 0:
            gs = jnp.concatenate([g_re * w_re + g_im * w_im, g_im * w_re - g_re * w_im], axis=1)
            sub = lax.broadcasted_iota(jnp.int32, (rows, CHUNK), 0)
            back = jnp.where(source_row - own == sub, 1.0, 0.0).astype(jnp.bfloat16)
            s_high, s_low = high_low(gs)
            mine[...] += dot(jnp.concatenate([back, back], axis=1), jnp.concatenate([s_high, s_low], axis=0))
        else:
            flip[...] = g.T
            turned = flip[pl.ds(pl.multiple_of(own, 8), rows), :]
            f_high, f_low = high_low(turned)
            mine[...] += dot(
                jnp.concatenate([f_high, f_high, f_low], axis=1),
                jnp.concatenate([q_high, q_low, q_high], axis=0),
            )

    per = CHUNK // LANES
    last = total // CHUNK - 1

    def fetch(c, slot):
        for e in range(0, CHUNK, 8):
            for x in range(2):
                for u in range(8):
                    row = table[ids[x, c * per + e // LANES, e % LANES + u]]
                    factor[(slot * 2 + x) * CHUNK + e + u] = row
            yield

    def push(c, slot):
        for e in range(0, CHUNK, GROUP):
            for u in range(GROUP):
                for order in range(2):
                    acc = accs[order % len(accs)]
                    x = order ^ side
                    r = ids[x, c * per + e // LANES, e % LANES + u]
                    acc[r] = acc[r] + grads[(slot * 2 + x) * CHUNK + e + u]
            yield

    def drain(steps):
        for _ in steps:
            pass

    def chunk(c, carry):
        slot = c & 1
        in_turn(
            [compute(x, c * CHUNK, slot) for x in range(2)],
            (fetch(jnp.minimum(c + 1, last), 1 - slot), CHUNK // 8),
            (push(jnp.maximum(c - 1, 0), 1 - slot), CHUNK // GROUP),
        )
        return carry

    def empty(i, carry):
        grads[pl.ds(2 * CHUNK + i * 8, 8)] = jnp.zeros((8, LANE_TILES, LANES), jnp.float32)
        return carry

    lax.fori_loop(0, 2 * CHUNK // 8, empty, 0)
    drain(fetch(0, 0))
    lax.fori_loop(0, last + 1, chunk, 0)
    drain(push(last, last % 2))

    ent_ref[:, :half] = mine[:, :half]
    ent_ref[:, half:] = mine[:, width : width + half]


def gradients(spec, relations, where, blocks_of):
    half, rows, shards, blocks, edges = spec
    dim, part_rows, width = 2 * half, rows * shards, LANE_TILES // 2 * LANES
    relation_count = relations.shape[0]
    group = shards * blocks
    total = group * edges // 2
    small = part_rows <= 256
    totals = 2 if small else 1
    smem = pl.BlockSpec(memory_space=pltpu.SMEM)
    vmem = pl.BlockSpec(memory_space=pltpu.VMEM)
    return pl.pallas_call(
        functools.partial(main_kernel, spec),
        in_specs=[smem, pl.BlockSpec(memory_space=pl.ANY), vmem],
        out_specs=(vmem,) * (totals + 1),
        out_shape=(
            *[pltpu.VMEM((relation_count, LANE_TILES, LANES), jnp.float32)] * totals,
            jax.ShapeDtypeStruct((rows, dim), jnp.float32),
        ),
        scratch_shapes=[
            pltpu.VMEM((2 * shards, LANES), jnp.int32),
            pltpu.SMEM((2 * shards, LANES), jnp.int32),
            pltpu.VMEM((2 * shards, -(-packing(half, rows, blocks, part_rows)[0] // 8) * 8, width), jnp.float32),
            pltpu.VMEM((dim, relation_count), jnp.float32),
            pltpu.VMEM((relation_count, LANE_TILES, LANES), jnp.float32),
            pltpu.VMEM((part_rows, 2 * width), jnp.float32),
            pltpu.VMEM((2, 3 * part_rows, 2 * width), jnp.bfloat16),
            pltpu.VMEM((2, 6 * width, part_rows), jnp.bfloat16),
            pltpu.VMEM((2, 2 * group, part_rows), jnp.bfloat16),
            pltpu.VMEM((2, 8, total + edges + LANES), jnp.float32),
            pltpu.VMEM((2, total // LANES, LANES), jnp.int32),
            pltpu.SMEM((2, total // LANES, LANES), jnp.int32),
            pltpu.VMEM((4 * CHUNK, LANE_TILES, LANES), jnp.float32),
            pltpu.VMEM((4 * CHUNK, LANE_TILES, LANES), jnp.float32),
            pltpu.VMEM((part_rows, CHUNK), jnp.float32),
            pltpu.VMEM((rows, 2 * width), jnp.float32),
            pltpu.SemaphoreType.DMA,
            pltpu.SemaphoreType.DMA((relation_count // STEP,)),
            pltpu.SemaphoreType.DMA,
        ],
        compiler_params=pltpu.CompilerParams(vmem_limit_bytes=(40 if small else 54) * 1024 * 1024),
        name="gradients",
    )(where, in_hbm(relations.T), in_vmem(blocks_of) if small else blocks_of)


def body(entities, relations, src_index, dst_index, rel_index, neg_index, counts, edge_weight):
    rows, dim = entities.shape
    blocks, edges = src_index.shape[1:]
    dom_count, shards = lax.axis_size("dom"), lax.axis_size("block")
    part_rows = rows * shards
    partner_bit = dom_count.bit_length() - 2
    block_bits = shards.bit_length() - 1
    other_bits = [bit for bit in range(dom_count.bit_length() - 1) if bit != partner_bit]

    block = packed(entities, counts, src_index, dst_index, rel_index, neg_index, edge_weight, part_rows)
    upper = [("block", bit) for bit in reversed(range(1, block_bits))]
    blocks_of = gather_all(block, upper, [("dom", partner_bit), ("block", 0)])
    where = jnp.stack([lax.axis_index("block"), (lax.axis_index("dom") >> partner_bit) & 1]).astype(jnp.int32)

    spec = (dim // 2, rows, shards, blocks, edges)
    *accs, entity_grad = gradients(spec, relations, where, blocks_of)
    return entity_grad, summed(accs, dim, other_bits).T


def solution(mesh):
    placed = (
        P(("dom", "block"), None),
        P(),
        P("dom", "block", None),
        P("dom", "block", None),
        P("dom", "block", None),
        P("dom", "block", None),
        P("dom", "block"),
        P("dom", "block", None),
    )
    return jax.shard_map(
        body,
        mesh=mesh,
        in_specs=placed,
        out_specs=(P(("dom", "block"), None), P()),
        check_vma=False,
    )
```

```python
import functools

import jax
import jax.numpy as jnp
from jax import lax
from jax.experimental import pallas as pl
from jax.experimental.pallas import tpu as pltpu
from jax.sharding import PartitionSpec as P

LANES = 128
CHUNK = 256
GROUP = 8
STEP = 512
PARTS = 4
LANE_TILES = 4
SMALL_BYTES = 16 * 1024 * 1024


def swap(x, axis, bit):
    count = lax.axis_size(axis)
    return lax.ppermute(x, axis, [(i, i ^ (1 << bit)) for i in range(count)])


def gather_all(x, upper, lower):
    while upper:
        stage, upper = upper[:2], upper[2:]
        others = [swap(x, *step) for step in stage]
        if len(stage) == 2:
            (axis, bit), (_, other) = stage
            count = lax.axis_size(axis)
            others.append(lax.ppermute(x, axis, [(i, i ^ (1 << bit) ^ (1 << other)) for i in range(count)]))
        x = jnp.concatenate([x] + others, axis=0)
    halves = list(jnp.split(x, 2))
    for k in range(2):
        others = [swap(halves[0], *lower[k]), swap(halves[1], *lower[1 - k])]
        halves = [jnp.concatenate(both, axis=0) for both in zip(halves, others)]
    return jnp.concatenate(halves, axis=0)


def block_index(j, x, bits):
    depth = bits - 1
    out = 0
    for stage in range(depth - 1):
        out = out | (((j >> (bits - 1 - stage)) & 1) << stage)
    half, low = (j >> 1) & 1, j & 1
    straight = (x << (depth - 1)) | (low << depth)
    crossed = (low << (depth - 1)) | (x << depth)
    return out | (half << (depth + 1)) | (straight + half * (crossed - straight))


def high_low(x):
    high = x.astype(jnp.bfloat16)
    return high, (x - high.astype(jnp.float32)).astype(jnp.bfloat16)


def dot(a, b):
    return jnp.dot(a, b, preferred_element_type=jnp.float32)


def packing(half, rows, blocks, part_rows):
    width = LANE_TILES // 2 * LANES
    count = 4 * blocks + blocks * (part_rows // width) + 1
    room = width - half
    pieces = -(-width // room)
    return count, room, pieces, max(2 * rows, -(-pieces * count // 8) * 8)


def pack_kernel(half, part_rows, counts, entities, src, dst, rel, neg, weight, out_ref):
    rows = entities.shape[0]
    blocks, edges = src.shape[1:]
    width, height = out_ref.shape[2], out_ref.shape[1]
    draws = neg.shape[2]
    data = [ids[0].astype(jnp.float32) for ids in (src, dst, rel)]
    slot = lax.broadcasted_iota(jnp.int32, (1, edges), 1)
    for i in range(blocks):
        data.append(jnp.where(slot < counts[0, i], weight[0, i : i + 1, :], 0.0))
    drawn = jnp.concatenate([neg[0], jnp.zeros((8 - blocks, draws), jnp.int32)], axis=0).astype(jnp.float32)
    drawn = drawn.T.astype(jnp.int32)
    lane = lax.broadcasted_iota(jnp.int32, (draws, part_rows), 1)
    for i in range(blocks):
        hits = jnp.where(drawn[:, i : i + 1] == lane, 1.0, 0.0).astype(jnp.bfloat16)
        times = dot(jnp.ones((8, draws), jnp.bfloat16), hits)[:1] / draws
        data += [times[:, low : low + width] for low in range(0, part_rows, width)]
    last = jnp.zeros((1, width), jnp.float32)
    for i in range(blocks):
        last = jnp.where(slot == i, counts[0, i].astype(jnp.float32), last)
    data = jnp.concatenate(data + [last], axis=0)
    count, room, pieces, _ = packing(half, rows, blocks, part_rows)
    cut = [pltpu.roll(data, (half - room * piece) % width, 1) for piece in range(pieces)]
    cut.append(jnp.zeros((height - pieces * count, width), jnp.float32))
    beside = jnp.concatenate(cut, axis=0)
    gap = jnp.zeros((2 * rows, width - half), jnp.float32)
    held = jnp.concatenate([entities[:, :half], entities[:, half:]], axis=0)
    held = jnp.concatenate([held, gap], axis=1)
    if height > 2 * rows:
        held = jnp.concatenate([held, jnp.zeros((height - 2 * rows, width), jnp.float32)], axis=0)
    out_ref[0] = jnp.where(lax.broadcasted_iota(jnp.int32, held.shape, 1) < half, held, beside)


def packed(entities, counts, src, dst, rel, neg, weight, part_rows):
    rows, dim = entities.shape
    width = LANE_TILES // 2 * LANES
    height = packing(dim // 2, rows, src.shape[1], part_rows)[3]
    vmem = pl.BlockSpec(memory_space=pltpu.VMEM)
    return pl.pallas_call(
        functools.partial(pack_kernel, dim // 2, part_rows),
        in_specs=[pl.BlockSpec(memory_space=pltpu.SMEM)] + [vmem] * 6,
        out_specs=vmem,
        out_shape=jax.ShapeDtypeStruct((1, height, width), jnp.float32),
        compiler_params=pltpu.CompilerParams(vmem_limit_bytes=SMALL_BYTES),
        name="pack",
    )(*[in_hbm(x) for x in (counts, entities, src, dst, rel, neg, weight)])


def in_vmem(x):
    return pltpu.with_memory_space_constraint(x, pltpu.VMEM)


def in_hbm(x):
    return pltpu.with_memory_space_constraint(x, pltpu.HBM)


def finish_kernel(half, low, *refs):
    accs, out_ref = refs[:-1], refs[-1]
    for i in range(out_ref.shape[1] // LANES):
        for q in range(LANE_TILES):
            rows = sum(tiles(acc, low + i * LANES, LANES, q) for acc in accs).T
            top = (q // 2) * half + (q % 2) * LANES
            size = min(LANES, half - (q % 2) * LANES)
            out_ref[top : top + size, i * LANES : (i + 1) * LANES] = rows[:size]


def add_kernel(one_ref, other_ref, *refs):
    refs[-1][...] = one_ref[...] + other_ref[...]


def summed(accs, dim, bits):
    count = accs[0].shape[0]
    size = count // PARTS
    parts = []
    for k in range(PARTS):
        part = pl.pallas_call(
            functools.partial(finish_kernel, dim // 2, k * size),
            in_specs=[pl.BlockSpec(memory_space=pltpu.VMEM)] * len(accs),
            out_specs=pl.BlockSpec(memory_space=pltpu.VMEM),
            out_shape=pltpu.VMEM((dim, size), jnp.float32),
            cost_estimate=pl.CostEstimate(flops=0, bytes_accessed=size * dim * 8, transcendentals=0),
            compiler_params=pltpu.CompilerParams(vmem_limit_bytes=SMALL_BYTES),
            name="turn",
        )(*[in_vmem(acc) for acc in accs])
        for bit in bits[:-1]:
            part = part + swap(part, "dom", bit)
        parts.append((part, swap(part, "dom", bits[-1])))
    total = None
    for k, (part, other) in enumerate(parts):
        block = pl.BlockSpec((dim, size), lambda i: (0, 0))
        total = pl.pallas_call(
            add_kernel,
            grid=(1,),
            in_specs=[block, block] + ([] if total is None else [pl.BlockSpec(memory_space=pl.ANY)]),
            out_specs=pl.BlockSpec((dim, size), lambda i, k=k: (0, k)),
            out_shape=jax.ShapeDtypeStruct((dim, count), jnp.float32),
            input_output_aliases={} if total is None else {2: 0},
            cost_estimate=pl.CostEstimate(flops=size * dim, bytes_accessed=size * dim * 12, transcendentals=0),
            compiler_params=pltpu.CompilerParams(vmem_limit_bytes=SMALL_BYTES),
            name="add_part",
        )(part, other, *([] if total is None else [total]))
    return total


def tiles(ref, low, count, q):
    flat = ref.reshape(ref.shape[0] * ref.shape[1], LANES)
    return flat[pl.ds(low * LANE_TILES + q, count, stride=LANE_TILES), :]


STAGES = 4
FIRST = 2
SCRATCH = 19


def in_turn(parts, *sides):
    for stage in range(STAGES):
        for part in parts:
            next(part, None)
            for side, steps in sides if stage >= FIRST else []:
                for _ in range(-(-steps // ((STAGES - FIRST) * len(parts)))):
                    next(side, None)


def main_kernel(spec, relations, blocks_of, *refs):
    accs, ent_ref, scratch = refs[:-SCRATCH][:-1], refs[:-SCRATCH][-1], refs[-SCRATCH:]
    half, rows, shards, blocks, edges, partner_bit = spec
    (live_v, live, data_rows, columns_of, table, ent, stack, stack_t, times, info, ids_v, ids, factor, grads, flip, mine, seg, come, known) = scratch
    width = LANE_TILES // 2 * LANES
    part_rows = rows * shards
    group = shards * blocks
    total = group * edges // 2
    bits = shards.bit_length() - 1
    count, room, pieces, _ = packing(half, rows, blocks, part_rows)
    me, side = lax.axis_index("block"), (lax.axis_index("dom") >> partner_bit) & 1
    own = me * rows

    steps = accs[0].shape[0] // STEP
    arrivals = []
    for k in range(steps):
        at = pl.ds(k * STEP, STEP)
        arrivals.append(pltpu.make_async_copy(relations.at[:, at], columns_of.at[:, at], come.at[k]))
        arrivals[-1].start()

    mine[...] = jnp.zeros_like(mine)
    info[...] = jnp.zeros_like(info)

    lane = lax.broadcasted_iota(jnp.int32, (count, width), 1)
    for k in range(2 * shards):
        raw = jnp.zeros((count, width), jnp.float32)
        for piece in range(pieces):
            square = blocks_of[k, piece * count : (piece + 1) * count, :]
            square = pltpu.roll(square, (room * piece - half) % width, 1)
            raw = jnp.where((lane >= room * piece) & (lane < room * (piece + 1)), square, raw)
        data_rows[k, :count, :] = raw
        live_v[k : k + 1, :] = raw[count - 1 :, :LANES].astype(jnp.int32)
    tell = pltpu.make_async_copy(live_v, live, known)
    tell.start()

    for x in range(2):
        for j in range(shards):
            k = block_index(j, x, bits)
            at = pl.ds(pl.multiple_of((j ^ me) * rows, 8), rows)
            lane = lax.broadcasted_iota(jnp.int32, (rows, width), 1)
            for part in range(2):
                square = blocks_of[k, part * rows : (part + 1) * rows, :]
                ent[at, part * width : (part + 1) * width] = jnp.where(lane < half, square, 0.0)
        whole = ent[...]
        high, low = high_low(whole)
        stack[x] = jnp.concatenate([high, low, high], axis=0)
        high, low = high_low(whole.T)
        stack_t[x] = jnp.concatenate([high, low, high], axis=0)

    tell.wait()

    for x in range(2):
        rows_of = []
        for n in range(group):
            k = block_index((n // blocks) ^ me, x, bits)
            low = 4 * blocks + (n % blocks) * (part_rows // width)
            whole = [data_rows[k, low + i : low + i + 1, :] for i in range(part_rows // width)]
            rows_of.append(jnp.concatenate(whole, axis=1))
        high, low = high_low(jnp.concatenate(rows_of, axis=0))
        times[x] = jnp.concatenate([high, low], axis=0)

        def lay(n, offset):
            k, slot = block_index((n // blocks) ^ me, x, bits), n % blocks
            alive = live[k, slot]
            tile = data_rows[k, : 4 * blocks, :]

            def chosen(k):
                row = tile[k * blocks : k * blocks + 1]
                for i in range(1, blocks):
                    row = jnp.where(slot == i, tile[k * blocks + i : k * blocks + i + 1], row)
                return row

            number = jnp.zeros((1, edges), jnp.float32) + n.astype(jnp.float32)
            data = [chosen(k) for k in range(4)] + [number, jnp.zeros((3, edges), jnp.float32)]
            data = jnp.concatenate(data, axis=0)
            data = jnp.where(lax.broadcasted_iota(jnp.int32, data.shape, 1) < alive, data, 0.0)
            data = jnp.concatenate([data, jnp.zeros((8, LANES), jnp.float32)], axis=1)
            data = pltpu.roll(data, offset % LANES, 1)
            at = pl.ds(pl.multiple_of((offset // LANES) * LANES, LANES), edges + LANES)
            info[x, :, at] = info[x, :, at] + data
            return offset + alive

        lax.fori_loop(0, group, lay, jnp.int32(0))
        for i in range(total // LANES):
            ids_v[x, i : i + 1, :] = info[x, 2:3, i * LANES : (i + 1) * LANES].astype(jnp.int32)

    move = pltpu.make_async_copy(ids_v, ids, seg)
    move.start()

    def turn(k, carry):
        low = k * STEP
        at = pl.ds(pl.multiple_of(low, STEP), STEP)
        pltpu.make_async_copy(relations.at[:, at], columns_of.at[:, at], come.at[k]).wait()
        flat = table.reshape(table.shape[0] * LANE_TILES, LANES)
        for part in range(2):
            square = columns_of[part * half : (part + 1) * half, at]
            square = jnp.concatenate([square, jnp.zeros((width - half, STEP), jnp.float32)], axis=0).T
            for j in range(LANE_TILES // 2):
                to = pl.ds(low * LANE_TILES + part * (LANE_TILES // 2) + j, STEP, stride=LANE_TILES)
                flat[to, :] = square[:, j * LANES : (j + 1) * LANES]
        to = pl.ds(pl.multiple_of(low * LANE_TILES, 8), STEP * LANE_TILES)
        for acc in accs:
            flat = acc.reshape(acc.shape[0] * LANE_TILES, LANES)
            flat[to, :] = jnp.zeros((STEP * LANE_TILES, LANES), jnp.float32)
        return carry

    lax.fori_loop(0, steps, turn, 0)
    move.wait()

    def row_id(x, at):
        return ids[x, at // LANES, at % LANES]

    def compute(x, start, slot):
        at = pl.ds(pl.multiple_of(start, CHUNK), CHUNK)
        data = info[x, :, at]
        columns = data.T
        source_row = data[0:1].astype(jnp.int32)
        source_col = columns[:, 0:1].astype(jnp.int32)
        target_col = columns[:, 1:2].astype(jnp.int32)
        weight_col = columns[:, 3:4]
        block_col = columns[:, 4:5].astype(jnp.int32)

        lane = lax.broadcasted_iota(jnp.int32, (CHUNK, part_rows), 1)
        pick = jnp.where(source_col == lane, 1.0, 0.0).astype(jnp.bfloat16)
        sources = dot(jnp.concatenate([pick, pick], axis=1), stack[x, : 2 * part_rows])
        yield
        s_re, s_im = sources[:, :width], sources[:, width:]
        w = [tiles(factor, (slot * 2 + x) * CHUNK, CHUNK, q) for q in range(LANE_TILES)]
        w_re, w_im = jnp.concatenate(w[:2], axis=1), jnp.concatenate(w[2:], axis=1)
        queries = jnp.concatenate([s_re * w_re - s_im * w_im, s_re * w_im + s_im * w_re], axis=1)
        q_high, q_low = high_low(queries)
        scores = dot(jnp.concatenate([q_high, q_high, q_low], axis=1), stack_t[1 - x])
        yield

        which = jnp.where(
            block_col == lax.broadcasted_iota(jnp.int32, (CHUNK, 2 * group), 1) % group, 1.0, 0.0
        ).astype(jnp.bfloat16)
        often = dot(which, times[x])

        sig = 1.0 / (1.0 + jnp.exp(-scores))
        sig_neg = 1.0 / (1.0 + jnp.exp(scores))
        g = sig * often - jnp.where(target_col == lane, sig_neg, 0.0)
        g = g * weight_col
        g_high, g_low = high_low(g)
        gq = dot(jnp.concatenate([g_high, g_high, g_low], axis=1), stack[1 - x])
        yield
        g_re, g_im = gq[:, :width], gq[:, width:]
        gw = jnp.concatenate([g_re * s_re + g_im * s_im, g_im * s_re - g_re * s_im], axis=1)
        flat = grads.reshape(4 * CHUNK * LANE_TILES, LANES)
        for q in range(LANE_TILES):
            at = pl.ds((slot * 2 + x) * CHUNK * LANE_TILES + q, CHUNK, stride=LANE_TILES)
            flat[at, :] = gw[:, q * LANES : (q + 1) * LANES]

        if x == 0:
            gs = jnp.concatenate([g_re * w_re + g_im * w_im, g_im * w_re - g_re * w_im], axis=1)
            sub = lax.broadcasted_iota(jnp.int32, (rows, CHUNK), 0)
            back = jnp.where(source_row - own == sub, 1.0, 0.0).astype(jnp.bfloat16)
            s_high, s_low = high_low(gs)
            mine[...] += dot(jnp.concatenate([back, back], axis=1), jnp.concatenate([s_high, s_low], axis=0))
        else:
            flip[...] = g.T
            turned = flip[pl.ds(pl.multiple_of(own, 8), rows), :]
            f_high, f_low = high_low(turned)
            mine[...] += dot(
                jnp.concatenate([f_high, f_high, f_low], axis=1),
                jnp.concatenate([q_high, q_low, q_high], axis=0),
            )

    per = CHUNK // LANES
    last = total // CHUNK - 1

    def fetch(c, slot):
        for e in range(0, CHUNK, 8):
            for x in range(2):
                for u in range(8):
                    row = table[ids[x, c * per + e // LANES, e % LANES + u]]
                    factor[(slot * 2 + x) * CHUNK + e + u] = row
            yield

    def push(c, slot):
        for e in range(0, CHUNK, GROUP):
            for u in range(GROUP):
                for order in range(2):
                    acc = accs[order % len(accs)]
                    x = order ^ side
                    r = ids[x, c * per + e // LANES, e % LANES + u]
                    acc[r] = acc[r] + grads[(slot * 2 + x) * CHUNK + e + u]
            yield

    def drain(steps):
        for _ in steps:
            pass

    def chunk(c, carry):
        slot = c & 1
        in_turn(
            [compute(x, c * CHUNK, slot) for x in range(2)],
            (fetch(jnp.minimum(c + 1, last), 1 - slot), CHUNK // 8),
            (push(jnp.maximum(c - 1, 0), 1 - slot), CHUNK // GROUP),
        )
        return carry

    def empty(i, carry):
        grads[pl.ds(2 * CHUNK + i * 8, 8)] = jnp.zeros((8, LANE_TILES, LANES), jnp.float32)
        return carry

    lax.fori_loop(0, 2 * CHUNK // 8, empty, 0)
    drain(fetch(0, 0))
    lax.fori_loop(0, last + 1, chunk, 0)
    drain(push(last, last % 2))

    ent_ref[:, :half] = mine[:, :half]
    ent_ref[:, half:] = mine[:, width : width + half]


def gradients(spec, relations, blocks_of):
    half, rows, shards, blocks, edges = spec[:5]
    dim, part_rows, width = 2 * half, rows * shards, LANE_TILES // 2 * LANES
    relation_count = relations.shape[0]
    group = shards * blocks
    total = group * edges // 2
    small = part_rows <= 256
    totals = 2 if small else 1
    vmem = pl.BlockSpec(memory_space=pltpu.VMEM)
    return pl.pallas_call(
        functools.partial(main_kernel, spec),
        in_specs=[pl.BlockSpec(memory_space=pl.ANY), vmem],
        out_specs=(vmem,) * (totals + 1),
        out_shape=(
            *[pltpu.VMEM((relation_count, LANE_TILES, LANES), jnp.float32)] * totals,
            jax.ShapeDtypeStruct((rows, dim), jnp.float32),
        ),
        scratch_shapes=[
            pltpu.VMEM((2 * shards, LANES), jnp.int32),
            pltpu.SMEM((2 * shards, LANES), jnp.int32),
            pltpu.VMEM((2 * shards, -(-packing(half, rows, blocks, part_rows)[0] // 8) * 8, width), jnp.float32),
            pltpu.VMEM((dim, relation_count), jnp.float32),
            pltpu.VMEM((relation_count, LANE_TILES, LANES), jnp.float32),
            pltpu.VMEM((part_rows, 2 * width), jnp.float32),
            pltpu.VMEM((2, 3 * part_rows, 2 * width), jnp.bfloat16),
            pltpu.VMEM((2, 6 * width, part_rows), jnp.bfloat16),
            pltpu.VMEM((2, 2 * group, part_rows), jnp.bfloat16),
            pltpu.VMEM((2, 8, total + edges + LANES), jnp.float32),
            pltpu.VMEM((2, total // LANES, LANES), jnp.int32),
            pltpu.SMEM((2, total // LANES, LANES), jnp.int32),
            pltpu.VMEM((4 * CHUNK, LANE_TILES, LANES), jnp.float32),
            pltpu.VMEM((4 * CHUNK, LANE_TILES, LANES), jnp.float32),
            pltpu.VMEM((part_rows, CHUNK), jnp.float32),
            pltpu.VMEM((rows, 2 * width), jnp.float32),
            pltpu.SemaphoreType.DMA,
            pltpu.SemaphoreType.DMA((relation_count // STEP,)),
            pltpu.SemaphoreType.DMA,
        ],
        compiler_params=pltpu.CompilerParams(vmem_limit_bytes=(40 if small else 54) * 1024 * 1024),
        name="gradients",
    )(in_hbm(relations.T), in_vmem(blocks_of) if small else blocks_of)


def body(entities, relations, src_index, dst_index, rel_index, neg_index, counts, edge_weight):
    rows, dim = entities.shape
    blocks, edges = src_index.shape[1:]
    dom_count, shards = lax.axis_size("dom"), lax.axis_size("block")
    part_rows = rows * shards
    partner_bit = dom_count.bit_length() - 2
    block_bits = shards.bit_length() - 1
    other_bits = [bit for bit in range(dom_count.bit_length() - 1) if bit != partner_bit]

    block = packed(entities, counts, src_index, dst_index, rel_index, neg_index, edge_weight, part_rows)
    upper = [("block", bit) for bit in reversed(range(1, block_bits))]
    blocks_of = gather_all(block, upper, [("dom", partner_bit), ("block", 0)])

    spec = (dim // 2, rows, shards, blocks, edges, partner_bit)
    *accs, entity_grad = gradients(spec, relations, blocks_of)
    return entity_grad, summed(accs, dim, other_bits).T


def solution(mesh):
    placed = (
        P(("dom", "block"), None),
        P(),
        P("dom", "block", None),
        P("dom", "block", None),
        P("dom", "block", None),
        P("dom", "block", None),
        P("dom", "block"),
        P("dom", "block", None),
    )
    return jax.shard_map(
        body,
        mesh=mesh,
        in_specs=placed,
        out_specs=(P(("dom", "block"), None), P()),
        check_vma=False,
    )
```

```python
import functools

import jax
import jax.numpy as jnp
from jax import lax
from jax.experimental import pallas as pl
from jax.experimental.pallas import tpu as pltpu
from jax.sharding import PartitionSpec as P

LANES = 128
CHUNK = 256
GROUP = 8
STEP = 512
PARTS = 4
LANE_TILES = 4
SMALL_BYTES = 16 * 1024 * 1024


def swap(x, axis, bit):
    count = lax.axis_size(axis)
    return lax.ppermute(x, axis, [(i, i ^ (1 << bit)) for i in range(count)])


def gather_all(x, upper, lower):
    while upper:
        stage, upper = upper[:2], upper[2:]
        others = [swap(x, *step) for step in stage]
        if len(stage) == 2:
            (axis, bit), (_, other) = stage
            count = lax.axis_size(axis)
            others.append(lax.ppermute(x, axis, [(i, i ^ (1 << bit) ^ (1 << other)) for i in range(count)]))
        x = jnp.concatenate([x] + others, axis=0)
    halves = list(jnp.split(x, 2))
    for k in range(2):
        others = [swap(halves[0], *lower[k]), swap(halves[1], *lower[1 - k])]
        halves = [jnp.concatenate(both, axis=0) for both in zip(halves, others)]
    return jnp.concatenate(halves, axis=0)


def block_index(j, x, bits):
    depth = bits - 1
    out = 0
    for stage in range(depth - 1):
        out = out | (((j >> (bits - 1 - stage)) & 1) << stage)
    half, low = (j >> 1) & 1, j & 1
    straight = (x << (depth - 1)) | (low << depth)
    crossed = (low << (depth - 1)) | (x << depth)
    return out | (half << (depth + 1)) | (straight + half * (crossed - straight))


def high_low(x):
    high = x.astype(jnp.bfloat16)
    return high, (x - high.astype(jnp.float32)).astype(jnp.bfloat16)


def dot(a, b):
    return jnp.dot(a, b, preferred_element_type=jnp.float32)


def packing(half, rows, blocks, part_rows):
    width = LANE_TILES // 2 * LANES
    count = 4 * blocks + blocks * (part_rows // width) + 1
    room = width - half
    pieces = -(-width // room)
    return count, room, pieces, max(2 * rows, -(-pieces * count // 8) * 8)


def pack_kernel(half, part_rows, counts, entities, src, dst, rel, neg, weight, out_ref):
    rows = entities.shape[0]
    blocks, edges = src.shape[1:]
    width, height = out_ref.shape[2], out_ref.shape[1]
    draws = neg.shape[2]
    data = [ids[0].astype(jnp.float32) for ids in (src, dst, rel)]
    slot = lax.broadcasted_iota(jnp.int32, (1, edges), 1)
    for i in range(blocks):
        data.append(jnp.where(slot < counts[0, i], weight[0, i : i + 1, :], 0.0))
    drawn = jnp.concatenate([neg[0], jnp.zeros((8 - blocks, draws), jnp.int32)], axis=0).astype(jnp.float32)
    drawn = drawn.T.astype(jnp.int32)
    lane = lax.broadcasted_iota(jnp.int32, (draws, part_rows), 1)
    for i in range(blocks):
        hits = jnp.where(drawn[:, i : i + 1] == lane, 1.0, 0.0).astype(jnp.bfloat16)
        times = dot(jnp.ones((8, draws), jnp.bfloat16), hits)[:1] / draws
        data += [times[:, low : low + width] for low in range(0, part_rows, width)]
    last = jnp.zeros((1, width), jnp.float32)
    for i in range(blocks):
        last = jnp.where(slot == i, counts[0, i].astype(jnp.float32), last)
    data = jnp.concatenate(data + [last], axis=0)
    count, room, pieces, _ = packing(half, rows, blocks, part_rows)
    cut = [pltpu.roll(data, (half - room * piece) % width, 1) for piece in range(pieces)]
    cut.append(jnp.zeros((height - pieces * count, width), jnp.float32))
    beside = jnp.concatenate(cut, axis=0)
    gap = jnp.zeros((2 * rows, width - half), jnp.float32)
    held = jnp.concatenate([entities[:, :half], entities[:, half:]], axis=0)
    held = jnp.concatenate([held, gap], axis=1)
    if height > 2 * rows:
        held = jnp.concatenate([held, jnp.zeros((height - 2 * rows, width), jnp.float32)], axis=0)
    out_ref[0] = jnp.where(lax.broadcasted_iota(jnp.int32, held.shape, 1) < half, held, beside)


def packed(entities, counts, src, dst, rel, neg, weight, part_rows):
    rows, dim = entities.shape
    width = LANE_TILES // 2 * LANES
    height = packing(dim // 2, rows, src.shape[1], part_rows)[3]
    vmem = pl.BlockSpec(memory_space=pltpu.VMEM)
    return pl.pallas_call(
        functools.partial(pack_kernel, dim // 2, part_rows),
        in_specs=[pl.BlockSpec(memory_space=pltpu.SMEM)] + [vmem] * 6,
        out_specs=vmem,
        out_shape=jax.ShapeDtypeStruct((1, height, width), jnp.float32),
        compiler_params=pltpu.CompilerParams(vmem_limit_bytes=SMALL_BYTES),
        name="pack",
    )(*[in_hbm(x) for x in (counts, entities, src, dst, rel, neg, weight)])


def in_vmem(x):
    return pltpu.with_memory_space_constraint(x, pltpu.VMEM)


def in_hbm(x):
    return pltpu.with_memory_space_constraint(x, pltpu.HBM)


def finish_kernel(half, low, *refs):
    accs, out_ref = refs[:-1], refs[-1]
    for i in range(out_ref.shape[1] // LANES):
        for q in range(LANE_TILES):
            rows = sum(tiles(acc, low + i * LANES, LANES, q) for acc in accs).T
            top = (q // 2) * half + (q % 2) * LANES
            size = min(LANES, half - (q % 2) * LANES)
            out_ref[top : top + size, i * LANES : (i + 1) * LANES] = rows[:size]


def add_kernel(one_ref, other_ref, *refs):
    refs[-1][...] = one_ref[...] + other_ref[...]


def summed(accs, dim, bits):
    count = accs[0].shape[0]
    size = count // PARTS
    parts = []
    for k in range(PARTS):
        part = pl.pallas_call(
            functools.partial(finish_kernel, dim // 2, k * size),
            in_specs=[pl.BlockSpec(memory_space=pltpu.VMEM)] * len(accs),
            out_specs=pl.BlockSpec(memory_space=pltpu.VMEM),
            out_shape=pltpu.VMEM((dim, size), jnp.float32),
            cost_estimate=pl.CostEstimate(flops=0, bytes_accessed=size * dim * 8, transcendentals=0),
            compiler_params=pltpu.CompilerParams(vmem_limit_bytes=SMALL_BYTES),
            name="turn",
        )(*[in_vmem(acc) for acc in accs])
        for bit in bits[:-1]:
            part = part + swap(part, "dom", bit)
        parts.append((part, swap(part, "dom", bits[-1])))
    total = None
    for k, (part, other) in enumerate(parts):
        block = pl.BlockSpec((dim, size), lambda i: (0, 0))
        total = pl.pallas_call(
            add_kernel,
            grid=(1,),
            in_specs=[block, block] + ([] if total is None else [pl.BlockSpec(memory_space=pl.ANY)]),
            out_specs=pl.BlockSpec((dim, size), lambda i, k=k: (0, k)),
            out_shape=jax.ShapeDtypeStruct((dim, count), jnp.float32),
            input_output_aliases={} if total is None else {2: 0},
            cost_estimate=pl.CostEstimate(flops=size * dim, bytes_accessed=size * dim * 12, transcendentals=0),
            compiler_params=pltpu.CompilerParams(vmem_limit_bytes=SMALL_BYTES),
            name="add_part",
        )(part, other, *([] if total is None else [total]))
    return total


def tiles(ref, low, count, q):
    flat = ref.reshape(ref.shape[0] * ref.shape[1], LANES)
    return flat[pl.ds(low * LANE_TILES + q, count, stride=LANE_TILES), :]


STAGES = 4
FIRST = 2
SCRATCH = 19


def in_turn(parts, *sides):
    for stage in range(STAGES):
        for part in parts:
            next(part, None)
            for side, steps in sides if stage >= FIRST else []:
                for _ in range(-(-steps // ((STAGES - FIRST) * len(parts)))):
                    next(side, None)


def main_kernel(spec, relations, blocks_of, *refs):
    accs, ent_ref, scratch = refs[:-SCRATCH][:-1], refs[:-SCRATCH][-1], refs[-SCRATCH:]
    half, rows, shards, blocks, edges, partner_bit = spec
    (live_v, live, data_rows, columns_of, table, ent, stack, stack_t, times, info, ids_v, ids, factor, grads, flip, mine, seg, come, known) = scratch
    width = LANE_TILES // 2 * LANES
    part_rows = rows * shards
    group = shards * blocks
    total = group * edges // 2
    bits = shards.bit_length() - 1
    count, room, pieces, _ = packing(half, rows, blocks, part_rows)
    me, side = lax.axis_index("block"), (lax.axis_index("dom") >> partner_bit) & 1
    own = me * rows

    steps = accs[0].shape[0] // STEP
    arrivals = []
    for k in range(steps):
        at = pl.ds(k * STEP, STEP)
        arrivals.append(pltpu.make_async_copy(relations.at[:, at], columns_of.at[:, at], come.at[k]))
        arrivals[-1].start()

    mine[...] = jnp.zeros_like(mine)
    info[...] = jnp.zeros_like(info)

    lane = lax.broadcasted_iota(jnp.int32, (count, width), 1)
    for k in range(2 * shards):
        raw = jnp.zeros((count, width), jnp.float32)
        for piece in range(pieces):
            square = blocks_of[k, piece * count : (piece + 1) * count, :]
            square = pltpu.roll(square, (room * piece - half) % width, 1)
            raw = jnp.where((lane >= room * piece) & (lane < room * (piece + 1)), square, raw)
        data_rows[k, :count, :] = raw
        live_v[k : k + 1, :] = raw[count - 1 :, :LANES].astype(jnp.int32)
    tell = pltpu.make_async_copy(live_v, live, known)
    tell.start()

    for x in range(2):
        for j in range(shards):
            k = block_index(j, x, bits)
            at = pl.ds(pl.multiple_of((j ^ me) * rows, 8), rows)
            lane = lax.broadcasted_iota(jnp.int32, (rows, width), 1)
            for part in range(2):
                square = blocks_of[k, part * rows : (part + 1) * rows, :]
                ent[at, part * width : (part + 1) * width] = jnp.where(lane < half, square, 0.0)
        whole = ent[...]
        high, low = high_low(whole)
        stack[x] = jnp.concatenate([high, low, high], axis=0)
        high, low = high_low(whole.T)
        stack_t[x] = jnp.concatenate([high, low, high], axis=0)

    tell.wait()

    for x in range(2):
        rows_of = []
        for n in range(group):
            k = block_index((n // blocks) ^ me, x, bits)
            low = 4 * blocks + (n % blocks) * (part_rows // width)
            whole = [data_rows[k, low + i : low + i + 1, :] for i in range(part_rows // width)]
            rows_of.append(jnp.concatenate(whole, axis=1))
        high, low = high_low(jnp.concatenate(rows_of, axis=0))
        times[x] = jnp.concatenate([high, low], axis=0)

        def lay(n, offset):
            k, slot = block_index((n // blocks) ^ me, x, bits), n % blocks
            alive = live[k, slot]
            tile = data_rows[k, : 4 * blocks, :]

            def chosen(k):
                row = tile[k * blocks : k * blocks + 1]
                for i in range(1, blocks):
                    row = jnp.where(slot == i, tile[k * blocks + i : k * blocks + i + 1], row)
                return row

            number = jnp.zeros((1, edges), jnp.float32) + n.astype(jnp.float32)
            data = [chosen(k) for k in range(4)] + [number, jnp.zeros((3, edges), jnp.float32)]
            data = jnp.concatenate(data, axis=0)
            data = jnp.where(lax.broadcasted_iota(jnp.int32, data.shape, 1) < alive, data, 0.0)
            data = jnp.concatenate([data, jnp.zeros((8, LANES), jnp.float32)], axis=1)
            data = pltpu.roll(data, offset % LANES, 1)
            at = pl.ds(pl.multiple_of((offset // LANES) * LANES, LANES), edges + LANES)
            info[x, :, at] = info[x, :, at] + data
            return offset + alive

        lax.fori_loop(0, group, lay, jnp.int32(0))
        for i in range(total // LANES):
            ids_v[x, i : i + 1, :] = info[x, 2:3, i * LANES : (i + 1) * LANES].astype(jnp.int32)

    move = pltpu.make_async_copy(ids_v, ids, seg)
    move.start()

    def turn(k, carry):
        low = k * STEP
        at = pl.ds(pl.multiple_of(low, STEP), STEP)
        pltpu.make_async_copy(relations.at[:, at], columns_of.at[:, at], come.at[k]).wait()
        flat = table.reshape(table.shape[0] * LANE_TILES, LANES)
        for part in range(2):
            square = columns_of[part * half : (part + 1) * half, at]
            square = jnp.concatenate([square, jnp.zeros((width - half, STEP), jnp.float32)], axis=0).T
            for j in range(LANE_TILES // 2):
                to = pl.ds(low * LANE_TILES + part * (LANE_TILES // 2) + j, STEP, stride=LANE_TILES)
                flat[to, :] = square[:, j * LANES : (j + 1) * LANES]
        to = pl.ds(pl.multiple_of(low * LANE_TILES, 8), STEP * LANE_TILES)
        for acc in accs:
            flat = acc.reshape(acc.shape[0] * LANE_TILES, LANES)
            flat[to, :] = jnp.zeros((STEP * LANE_TILES, LANES), jnp.float32)
        return carry

    lax.fori_loop(0, steps, turn, 0)
    move.wait()

    def row_id(x, at):
        return ids[x, at // LANES, at % LANES]

    def compute(x, start, slot):
        at = pl.ds(pl.multiple_of(start, CHUNK), CHUNK)
        data = info[x, :, at]
        columns = data.T
        source_row = data[0:1].astype(jnp.int32)
        source_col = columns[:, 0:1].astype(jnp.int32)
        target_col = columns[:, 1:2].astype(jnp.int32)
        weight_col = columns[:, 3:4]
        block_col = columns[:, 4:5].astype(jnp.int32)

        lane = lax.broadcasted_iota(jnp.int32, (CHUNK, part_rows), 1)
        pick = jnp.where(source_col == lane, 1.0, 0.0).astype(jnp.bfloat16)
        sources = dot(jnp.concatenate([pick, pick], axis=1), stack[x, : 2 * part_rows])
        yield
        s_re, s_im = sources[:, :width], sources[:, width:]
        w = [tiles(factor, (slot * 2 + x) * CHUNK, CHUNK, q) for q in range(LANE_TILES)]
        w_re, w_im = jnp.concatenate(w[:2], axis=1), jnp.concatenate(w[2:], axis=1)
        queries = jnp.concatenate([s_re * w_re - s_im * w_im, s_re * w_im + s_im * w_re], axis=1)
        q_high, q_low = high_low(queries)
        scores = dot(jnp.concatenate([q_high, q_high, q_low], axis=1), stack_t[1 - x])
        yield

        which = jnp.where(
            block_col == lax.broadcasted_iota(jnp.int32, (CHUNK, 2 * group), 1) % group, 1.0, 0.0
        ).astype(jnp.bfloat16)
        often = dot(which, times[x])

        sig = 1.0 / (1.0 + jnp.exp(-scores))
        positive = jnp.sum(jnp.where(target_col == lane, scores, 0.0), axis=1, keepdims=True)
        sig_neg = 1.0 / (1.0 + jnp.exp(positive))
        g = sig * often - jnp.where(target_col == lane, sig_neg, 0.0)
        g = g * weight_col
        g_high, g_low = high_low(g)
        gq = dot(jnp.concatenate([g_high, g_high, g_low], axis=1), stack[1 - x])
        yield
        g_re, g_im = gq[:, :width], gq[:, width:]
        gw = jnp.concatenate([g_re * s_re + g_im * s_im, g_im * s_re - g_re * s_im], axis=1)
        flat = grads.reshape(4 * CHUNK * LANE_TILES, LANES)
        for q in range(LANE_TILES):
            at = pl.ds((slot * 2 + x) * CHUNK * LANE_TILES + q, CHUNK, stride=LANE_TILES)
            flat[at, :] = gw[:, q * LANES : (q + 1) * LANES]

        if x == 0:
            gs = jnp.concatenate([g_re * w_re + g_im * w_im, g_im * w_re - g_re * w_im], axis=1)
            sub = lax.broadcasted_iota(jnp.int32, (rows, CHUNK), 0)
            back = jnp.where(source_row - own == sub, 1.0, 0.0).astype(jnp.bfloat16)
            s_high, s_low = high_low(gs)
            mine[...] += dot(jnp.concatenate([back, back], axis=1), jnp.concatenate([s_high, s_low], axis=0))
        else:
            flip[...] = g.T
            turned = flip[pl.ds(pl.multiple_of(own, 8), rows), :]
            f_high, f_low = high_low(turned)
            mine[...] += dot(
                jnp.concatenate([f_high, f_high, f_low], axis=1),
                jnp.concatenate([q_high, q_low, q_high], axis=0),
            )

    per = CHUNK // LANES
    last = total // CHUNK - 1

    def fetch(c, slot):
        for e in range(0, CHUNK, 8):
            for x in range(2):
                for u in range(8):
                    row = table[ids[x, c * per + e // LANES, e % LANES + u]]
                    factor[(slot * 2 + x) * CHUNK + e + u] = row
            yield

    def push(c, slot):
        for e in range(0, CHUNK, GROUP):
            for u in range(GROUP):
                for order in range(2):
                    acc = accs[order % len(accs)]
                    x = order ^ side
                    r = ids[x, c * per + e // LANES, e % LANES + u]
                    acc[r] = acc[r] + grads[(slot * 2 + x) * CHUNK + e + u]
            yield

    def drain(steps):
        for _ in steps:
            pass

    def chunk(c, carry):
        slot = c & 1
        in_turn(
            [compute(x, c * CHUNK, slot) for x in range(2)],
            (fetch(jnp.minimum(c + 1, last), 1 - slot), CHUNK // 8),
            (push(jnp.maximum(c - 1, 0), 1 - slot), CHUNK // GROUP),
        )
        return carry

    def empty(i, carry):
        grads[pl.ds(2 * CHUNK + i * 8, 8)] = jnp.zeros((8, LANE_TILES, LANES), jnp.float32)
        return carry

    lax.fori_loop(0, 2 * CHUNK // 8, empty, 0)
    drain(fetch(0, 0))
    lax.fori_loop(0, last + 1, chunk, 0)
    drain(push(last, last % 2))

    ent_ref[:, :half] = mine[:, :half]
    ent_ref[:, half:] = mine[:, width : width + half]


def gradients(spec, relations, blocks_of):
    half, rows, shards, blocks, edges = spec[:5]
    dim, part_rows, width = 2 * half, rows * shards, LANE_TILES // 2 * LANES
    relation_count = relations.shape[0]
    group = shards * blocks
    total = group * edges // 2
    small = part_rows <= 256
    totals = 2 if small else 1
    vmem = pl.BlockSpec(memory_space=pltpu.VMEM)
    return pl.pallas_call(
        functools.partial(main_kernel, spec),
        in_specs=[pl.BlockSpec(memory_space=pl.ANY), vmem],
        out_specs=(vmem,) * (totals + 1),
        out_shape=(
            *[pltpu.VMEM((relation_count, LANE_TILES, LANES), jnp.float32)] * totals,
            jax.ShapeDtypeStruct((rows, dim), jnp.float32),
        ),
        scratch_shapes=[
            pltpu.VMEM((2 * shards, LANES), jnp.int32),
            pltpu.SMEM((2 * shards, LANES), jnp.int32),
            pltpu.VMEM((2 * shards, -(-packing(half, rows, blocks, part_rows)[0] // 8) * 8, width), jnp.float32),
            pltpu.VMEM((dim, relation_count), jnp.float32),
            pltpu.VMEM((relation_count, LANE_TILES, LANES), jnp.float32),
            pltpu.VMEM((part_rows, 2 * width), jnp.float32),
            pltpu.VMEM((2, 3 * part_rows, 2 * width), jnp.bfloat16),
            pltpu.VMEM((2, 6 * width, part_rows), jnp.bfloat16),
            pltpu.VMEM((2, 2 * group, part_rows), jnp.bfloat16),
            pltpu.VMEM((2, 8, total + edges + LANES), jnp.float32),
            pltpu.VMEM((2, total // LANES, LANES), jnp.int32),
            pltpu.SMEM((2, total // LANES, LANES), jnp.int32),
            pltpu.VMEM((4 * CHUNK, LANE_TILES, LANES), jnp.float32),
            pltpu.VMEM((4 * CHUNK, LANE_TILES, LANES), jnp.float32),
            pltpu.VMEM((part_rows, CHUNK), jnp.float32),
            pltpu.VMEM((rows, 2 * width), jnp.float32),
            pltpu.SemaphoreType.DMA,
            pltpu.SemaphoreType.DMA((relation_count // STEP,)),
            pltpu.SemaphoreType.DMA,
        ],
        compiler_params=pltpu.CompilerParams(vmem_limit_bytes=(40 if small else 54) * 1024 * 1024),
        name="gradients",
    )(in_hbm(relations.T), in_vmem(blocks_of) if small else blocks_of)


def body(entities, relations, src_index, dst_index, rel_index, neg_index, counts, edge_weight):
    rows, dim = entities.shape
    blocks, edges = src_index.shape[1:]
    dom_count, shards = lax.axis_size("dom"), lax.axis_size("block")
    part_rows = rows * shards
    partner_bit = dom_count.bit_length() - 2
    block_bits = shards.bit_length() - 1
    other_bits = [bit for bit in range(dom_count.bit_length() - 1) if bit != partner_bit]

    block = packed(entities, counts, src_index, dst_index, rel_index, neg_index, edge_weight, part_rows)
    upper = [("block", bit) for bit in reversed(range(1, block_bits))]
    blocks_of = gather_all(block, upper, [("dom", partner_bit), ("block", 0)])

    spec = (dim // 2, rows, shards, blocks, edges, partner_bit)
    *accs, entity_grad = gradients(spec, relations, blocks_of)
    return entity_grad, summed(accs, dim, other_bits).T


def solution(mesh):
    placed = (
        P(("dom", "block"), None),
        P(),
        P("dom", "block", None),
        P("dom", "block", None),
        P("dom", "block", None),
        P("dom", "block", None),
        P("dom", "block"),
        P("dom", "block", None),
    )
    return jax.shard_map(
        body,
        mesh=mesh,
        in_specs=placed,
        out_specs=(P(("dom", "block"), None), P()),
        check_vma=False,
    )
```
